32 devices in a mesh: rep: 4 (over x, core), dp: 8 (over z, y).
Axes of the slice: x: 2, y: 2, z: 4, core: 2. Of those that a mesh axis runs over, the one named last changes fastest.
Arguments:
- image_features: bfloat16 [4096, 1408], P(('rep', 'dp')), parts along dimension 0, may hold values from -24 to 24
- text_embed: bfloat16 [4096, 512], P(('rep', 'dp')), parts along dimension 0, may hold values from -24 to 24
- image_head: bfloat16 [5632, 512], P(('rep', 'dp')), parts along dimension 0, may hold values from -1 to 3
- logit_scale: float32 [1], replicated, may hold values from 10 to 40
Outputs:
- image_features_grad: bfloat16 [4096, 1408], P(('rep', 'dp')), parts along dimension 0
- text_embed_grad: bfloat16 [4096, 512], P(('rep', 'dp')), parts along dimension 0
- image_head_grad: float32 [5632, 512], P(('rep', 'dp')), parts along dimension 0
The draws below stay inside these ranges and needn't reach their ends.
There are 4 independent parts, one for each index of `rep`. The reference program is written for one: setup_inputs(seed, part) draws one part's arguments, and reference() takes and returns one part's arrays. A program takes and returns all parts, laid end to end along the dimension named above; an argument that names none is the same for every part. Nothing has to cross between parts.
All inputs are finite; a program needn't handle non-finite values.
Results may differ from the reference program's by a relative error of at most 0.02.
Values may be sent and summed in bfloat16 or wider, within the bound.
A program may use at most 64 MiB of HBM per device.

```python
import math
import jax
import jax.numpy as jnp
from jax import lax

DI = 1408
E = 512
B = 1024
N_DP = 8


def noise_block(key, shape):
    return jax.random.normal(key, shape, jnp.float32)


def latent_rows(key):
    base = jax.random.fold_in(key, 4101)
    topic_key, center_key, pull_key, own_key = jax.random.split(base, 4)
    topics = max(B // 16, 4)
    topic_ids = jax.random.randint(topic_key, (B,), 0, topics)
    centers = jax.random.normal(center_key, (topics, E), jnp.float32)
    pull = jnp.exp(jax.random.uniform(pull_key, (B, 1), jnp.float32, math.log(0.3), math.log(3.0)))
    return pull * centers[topic_ids] + noise_block(own_key, (B, E))


def draw_text_embed(key, part):
    latent = latent_rows(key)
    values = latent + 0.5 * noise_block(jax.random.fold_in(key, 4102), (B, E))
    return jnp.clip(values, -24.0, 24.0).astype(jnp.bfloat16)


def draw_image_features(key, part):
    latent = latent_rows(key)
    leading = latent + 0.5 * noise_block(jax.random.fold_in(key, 4104), (B, E))
    trailing = noise_block(jax.random.fold_in(key, 4105), (B, DI - E))
    values = jnp.concatenate([leading, trailing], axis=1)
    return jnp.clip(values, -24.0, 24.0).astype(jnp.bfloat16)


def draw_image_head(key, part):
    bound = 4.0 / math.sqrt(DI)
    noise = noise_block(jax.random.fold_in(key, 4107), (DI, E)) / math.sqrt(DI)
    noise = jnp.clip(noise, -bound, bound)
    row_ids = jax.lax.broadcasted_iota(jnp.int32, (DI, E), 0)
    col_ids = jax.lax.broadcasted_iota(jnp.int32, (DI, E), 1)
    diagonal = jnp.where(row_ids == col_ids, 2.0, 0.0).astype(jnp.float32)
    return (diagonal + noise).astype(jnp.bfloat16)


def setup_inputs(seed: int = 0, part: int = 0) -> dict:
    keys = jax.random.split(jax.random.key(seed), 5)
    part_keys = jax.random.split(jax.random.fold_in(keys[4], part), 5)
    image_features = draw_image_features(jax.random.fold_in(jax.random.fold_in(keys[4], part), 71), part)
    text_embed = draw_text_embed(jax.random.fold_in(jax.random.fold_in(keys[4], part), 71), part)
    image_head = draw_image_head(jax.random.fold_in(jax.random.fold_in(keys[4], part), 71), part)
    logit_scale = jnp.clip(jnp.exp(jax.random.uniform(keys[3], (1,), jnp.float32, math.log(10.0), math.log(40.0))), 10.0, 40.0)
    return dict(image_features=image_features, text_embed=text_embed, image_head=image_head, logit_scale=logit_scale)


def unit_rows(embedding):
    inv_norm = lax.rsqrt(lax.optimization_barrier(jnp.sum(embedding * embedding, axis=1, keepdims=True)) + 1e-06)
    return (embedding * inv_norm, inv_norm)

def norm_backward(embedding, inv_norm, upstream):
    inner = lax.optimization_barrier(jnp.sum(embedding * upstream, axis=1, keepdims=True))
    return (inv_norm * upstream - embedding * (inv_norm * inv_norm * inv_norm) * inner).astype(jnp.bfloat16)

def reference(image_features, text_embed, image_head, logit_scale):
    logit_mult = logit_scale[0]
    img_emb = jnp.dot(image_features, image_head, preferred_element_type=jnp.float32)
    img_scaled, img_inv = unit_rows(img_emb)
    img_unit = img_scaled.astype(jnp.bfloat16)
    txt_emb = text_embed.astype(jnp.float32)
    txt_scaled, txt_inv = unit_rows(txt_emb)
    txt_unit = txt_scaled.astype(jnp.bfloat16)
    logits = logit_mult * jnp.dot(img_unit, txt_unit.T, preferred_element_type=jnp.float32)
    row_lse = jnp.log(lax.optimization_barrier(jnp.sum(jnp.exp(logits), axis=1)))
    col_lse = jnp.log(lax.optimization_barrier(jnp.sum(jnp.exp(logits), axis=0)))
    eye_matrix = jnp.eye(logits.shape[0], dtype=jnp.float32)
    pair_weights = (jnp.exp(logits - row_lse[:, None]) + jnp.exp(logits - col_lse[None, :]) - 2.0 * eye_matrix).astype(jnp.bfloat16)
    img_unit_grad = logit_mult * jnp.dot(pair_weights, txt_unit, preferred_element_type=jnp.float32)
    txt_unit_grad = logit_mult * jnp.dot(pair_weights.T, img_unit, preferred_element_type=jnp.float32)
    img_emb_grad = norm_backward(img_emb, img_inv, img_unit_grad)
    text_embed_grad = norm_backward(txt_emb, txt_inv, txt_unit_grad)
    image_features_grad = jnp.dot(img_emb_grad, image_head.T, preferred_element_type=jnp.float32).astype(jnp.bfloat16)
    feats_blocks = image_features.reshape(N_DP, -1, DI).astype(jnp.float32)
    grad_blocks = img_emb_grad.reshape(N_DP, -1, E).astype(jnp.float32)
    partials = jnp.einsum('kbi,kbe->kie', feats_blocks, grad_blocks)
    partials = lax.optimization_barrier(partials.astype(jnp.bfloat16)).astype(jnp.float32)
    image_head_grad = lax.optimization_barrier(jnp.sum(partials, axis=0))
    return (image_features_grad, text_embed_grad, image_head_grad)
```

```python
import functools

import jax
import jax.numpy as jnp
from jax import lax
from jax.experimental import pallas as pl
from jax.experimental.pallas import tpu as pltpu
from jax.sharding import PartitionSpec as P


def unit_rows(embedding):
    inv_norm = lax.rsqrt(jnp.sum(embedding * embedding, axis=1, keepdims=True) + 1e-06)
    return (embedding * inv_norm, inv_norm)


def norm_backward(embedding, inv_norm, upstream):
    inner = jnp.sum(embedding * upstream, axis=1, keepdims=True)
    return (inv_norm * upstream - embedding * (inv_norm * inv_norm * inv_norm) * inner).astype(
        jnp.bfloat16
    )


def tile_logits(logit_mult, left_rows, right_rows):
    product = lax.dot_general(
        left_rows, right_rows, (((1,), (1,)), ((), ())), preferred_element_type=jnp.float32
    )
    return logit_mult * product


def pair_coef(logits, left_lse, right_lse, left_ids, right_ids):
    label = (left_ids[:, None] == right_ids[None, :]).astype(jnp.float32)
    values = (
        jnp.exp(logits - left_lse[:, None]) + jnp.exp(logits - right_lse[None, :]) - 2.0 * label
    )
    return values.astype(jnp.bfloat16)


def local(image_features, text_embed, image_head, logit_scale):
    logit_mult = logit_scale[0]
    row_count = image_features.shape[0]
    own_ids = lax.axis_index("dp") * row_count + jnp.arange(row_count, dtype=jnp.int32)
    head_full = lax.all_gather(image_head, "dp", axis=0, tiled=True)
    img_emb = jnp.dot(image_features, head_full, preferred_element_type=jnp.float32)
    img_scaled, img_inv = unit_rows(img_emb)
    img_unit = img_scaled.astype(jnp.bfloat16)
    txt_emb = text_embed.astype(jnp.float32)
    txt_scaled, txt_inv = unit_rows(txt_emb)
    txt_unit = txt_scaled.astype(jnp.bfloat16)
    exp_tile = jnp.exp(
        tile_logits(logit_mult, img_unit, lax.all_gather(txt_unit, "dp", axis=0, tiled=True))
    )
    col_part = jnp.sum(exp_tile, axis=0)
    row_sum, col_part = (jnp.sum(exp_tile, axis=1), col_part)
    row_lse = jnp.log(row_sum)
    col_lse = jnp.log(lax.psum_scatter(col_part, "dp", scatter_dimension=0, tiled=True))
    row_all, col_all = (
        lax.all_gather(row_lse, "dp", axis=0, tiled=True),
        lax.all_gather(col_lse, "dp", axis=0, tiled=True),
    )
    img_piece = lax.all_gather(img_unit, "dp", axis=0, tiled=True)
    txt_piece = lax.all_gather(txt_unit, "dp", axis=0, tiled=True)
    count = img_piece.shape[0]
    piece_ids = jnp.arange(count, dtype=jnp.int32)
    img_coef = pair_coef(
        tile_logits(logit_mult, img_unit, txt_piece), row_lse, col_all, own_ids, piece_ids
    )
    txt_coef = pair_coef(
        tile_logits(logit_mult, txt_unit, img_piece), col_lse, row_all, own_ids, piece_ids
    )
    img_acc = jnp.dot(img_coef, txt_piece, preferred_element_type=jnp.float32)
    txt_acc = jnp.dot(txt_coef, img_piece, preferred_element_type=jnp.float32)
    img_unit_grad = logit_mult * img_acc
    txt_unit_grad = logit_mult * txt_acc
    img_emb_grad = norm_backward(img_emb, img_inv, img_unit_grad)
    text_embed_grad = norm_backward(txt_emb, txt_inv, txt_unit_grad)
    image_features_grad = lax.dot_general(
        img_emb_grad, head_full, (((1,), (1,)), ((), ())), preferred_element_type=jnp.float32
    ).astype(jnp.bfloat16)
    head_partial = lax.dot_general(
        image_features, img_emb_grad, (((0,), (0,)), ((), ())), preferred_element_type=jnp.float32
    )
    image_head_grad = lax.psum_scatter(
        head_partial.astype(jnp.bfloat16), "dp", scatter_dimension=0, tiled=True
    ).astype(jnp.float32)
    return (image_features_grad, text_embed_grad, image_head_grad)


MESH = pl.DeviceIdType.MESH
HEAD, TEXT, IMAGE, GRAD = range(4)
ROWS_ROWS = (((1,), (1,)), ((), ()))
COLS_COLS = (((0,), (0,)), ((), ()))


def place_of(index, n):
    depth, side = lax.div(index, 2), lax.rem(index, 2)
    return depth + side * (n - 1 - 2 * depth)


def index_at(place, n):
    place = lax.rem(place + 2 * n, n)
    side = lax.div(place, n // 2)
    return 2 * (place + side * (n - 1 - 2 * place)) + side


def step_kernel(
    n,
    feat_ref,
    text_ref,
    head_ref,
    scale_ref,
    feat_grad_ref,
    text_grad_ref,
    head_grad_ref,
    head_all,
    text_all,
    image_all,
    feat_blocks,
    feat_t_blocks,
    exp_all,
    inv_rows,
    inv_cols,
    outgoing,
    incoming,
    send_sem,
    recv_sem,
):
    rows, width = text_ref.shape
    depth = head_ref.shape[0]
    half = width // 2
    messages = n - 1
    me = lax.axis_index("dp")
    place = place_of(me, n)
    partner = {+1: index_at(place + 1, n), -1: index_at(place - 1, n)}

    barrier = pltpu.get_barrier_semaphore()
    for way in (1, -1):
        pl.semaphore_signal(barrier, inc=1, device_id={"dp": partner[way]}, device_id_type=MESH)

    head_all[pl.ds(pl.multiple_of(me * depth, 16), depth), :] = head_ref[...]
    pl.semaphore_wait(barrier, 2)

    def columns(way, m):
        first = (m % 2 == 0) == (way == 1)
        return pl.ds(0 if first else half, half)

    def remote(kind, way, m, src, dst):
        side = 0 if way == 1 else 1
        return pltpu.make_async_remote_copy(
            src_ref=src,
            dst_ref=dst,
            send_sem=send_sem.at[kind, side, m],
            recv_sem=recv_sem.at[kind, side, m],
            device_id={"dp": partner[way]},
            device_id_type=MESH,
        )

    gathered = {HEAD: (head_all, depth), TEXT: (text_all, rows), IMAGE: (image_all, rows)}

    def gather_copy(kind, way, m, origin_shift):
        buf, block = gathered[kind]
        owner = index_at(place - way * origin_shift, n)
        ref = buf.at[pl.ds(pl.multiple_of(owner * block, 16), block), columns(way, m)]
        return remote(kind, way, m, ref, ref)

    def gather_send(kind, m):
        for way in (1, -1):
            if m >= 2:
                gather_copy(kind, way, m - 2, m // 2).wait_recv()
            gather_copy(kind, way, m, m // 2).start()

    def gather_last(kind):
        for m in range(max(messages - 2, 0), messages):
            for way in (1, -1):
                gather_copy(kind, way, m, m // 2 + 1).wait_recv()

    gather_send(HEAD, 0)
    gather_send(HEAD, 1)

    txt_emb = text_ref[...].astype(jnp.float32)
    txt_scaled, txt_inv = unit_rows(txt_emb)
    text_all[pl.ds(pl.multiple_of(me * rows, 16), rows), :] = txt_scaled.astype(jnp.bfloat16)
    feat_t = feat_ref[...].astype(jnp.float32).T
    for b in range(n):
        block = feat_t[b * depth : (b + 1) * depth]
        feat_t_blocks[b] = block.astype(jnp.bfloat16)
        feat_blocks[b] = block.T.astype(jnp.bfloat16)

    def emb_part(owner):
        return jnp.dot(
            feat_blocks[owner],
            head_all[pl.ds(pl.multiple_of(owner * depth, 16), depth), :],
            preferred_element_type=jnp.float32,
        )

    img_emb = emb_part(me)
    for m in range(2, messages):
        gather_send(HEAD, m)
        if m % 2 == 1:
            for way in (1, -1):
                img_emb += emb_part(index_at(place - way * (m // 2), n))
    gather_send(TEXT, 0)
    gather_send(TEXT, 1)
    gather_last(HEAD)
    for way in (1, -1):
        img_emb += emb_part(index_at(place - way * (n // 2 - 1), n))
    img_emb += emb_part(index_at(place + n // 2, n))
    img_scaled, img_inv = unit_rows(img_emb)
    image_all[pl.ds(pl.multiple_of(me * rows, 16), rows), :] = img_scaled.astype(jnp.bfloat16)

    for m in range(messages - 2):
        gather_send(IMAGE, m)
        gather_send(TEXT, m + 2)
    gather_last(TEXT)

    scale = scale_ref[0]

    def exp_block(owner, col_sum):
        at = pl.ds(pl.multiple_of(owner * rows, 16), rows)
        values = jnp.exp(
            scale
            * lax.dot_general(
                image_all[at, :], text_all[...], ROWS_ROWS, preferred_element_type=jnp.float32
            )
        )
        exp_all[at, :] = values
        inv_rows[at, :] = 1.0 / jnp.sum(values, axis=1, keepdims=True)
        return col_sum + jnp.sum(values, axis=0, keepdims=True)

    col_sum = exp_block(me, jnp.zeros((1, n * rows), jnp.float32))
    for shift in range(1, n // 2):
        m = messages - 2 + (shift - 1)
        if m < messages:
            gather_send(IMAGE, m)
        if shift == n // 2 - 1:
            gather_last(IMAGE)
        for way in (1, -1):
            col_sum = exp_block(index_at(place - way * shift, n), col_sum)
    col_sum = exp_block(index_at(place + n // 2, n), col_sum)
    inv_col = 1.0 / col_sum
    inv_cols[...] = inv_col

    own = pl.ds(pl.multiple_of(me * rows, 128), rows)
    pairs = n * rows
    row_ids = lax.broadcasted_iota(jnp.int32, (rows, pairs), 0) + me * rows
    label = (row_ids == lax.broadcasted_iota(jnp.int32, (rows, pairs), 1)).astype(jnp.float32)
    img_coef = exp_all[own, :] * (inv_rows[own, :] + inv_col) - 2.0 * label
    img_acc = jnp.dot(
        img_coef.astype(jnp.bfloat16), text_all[...], preferred_element_type=jnp.float32
    )
    img_emb_grad = norm_backward(img_emb, img_inv, scale * img_acc)

    def head_part(owner, cols):
        return jnp.dot(
            feat_t_blocks[owner],
            img_emb_grad[:, cols.start : cols.start + half],
            preferred_element_type=jnp.float32,
        )

    def grad_copy(way, m):
        side = 0 if way == 1 else 1
        return remote(GRAD, way, m, outgoing.at[side, m], incoming.at[side, m])

    def grad_send(m):
        for way in (1, -1):
            side = 0 if way == 1 else 1
            value = head_part(index_at(place + way * (n // 2 - (m + 1) // 2), n), columns(way, m))
            if m >= 2:
                grad_copy(way, m - 2).wait_recv()
                value += incoming[side, m - 2].astype(jnp.float32)
            outgoing[side, m] = value.astype(jnp.bfloat16)
            grad_copy(way, m).start()

    def text_side():
        row_ids = lax.broadcasted_iota(jnp.int32, (pairs, rows), 0)
        col_ids = lax.broadcasted_iota(jnp.int32, (pairs, rows), 1) + me * rows
        label = (row_ids == col_ids).astype(jnp.float32)
        coef = exp_all[:, own] * (inv_rows[...] + inv_cols[:, own]) - 2.0 * label
        acc = lax.dot_general(
            coef.astype(jnp.bfloat16), image_all[...], COLS_COLS, preferred_element_type=jnp.float32
        )
        text_grad_ref[...] = norm_backward(txt_emb, txt_inv, scale * acc)

    def feat_side():
        feat_grad_ref[...] = lax.dot_general(
            img_emb_grad, head_all[...], ROWS_ROWS, preferred_element_type=jnp.float32
        ).astype(jnp.bfloat16)

    for m in range(messages):
        grad_send(m)
        if m == 1:
            text_side()
        if m == 3:
            feat_side()

    total = [head_part(me, pl.ds(0, half)), head_part(me, pl.ds(half, half))]
    for m in range(messages - 2, messages):
        for way in (1, -1):
            grad_copy(way, m).wait_recv()
            which = columns(way, m).start // half
            total[which] += incoming[0 if way == 1 else 1, m].astype(jnp.float32)
    head_grad_ref[:, 0:half] = total[0]
    head_grad_ref[:, half:width] = total[1]

    for m in range(messages):
        for way in (1, -1):
            for kind in gathered:
                gather_copy(kind, way, m, m // 2).wait_send()
            grad_copy(way, m).wait_send()


def local_kernel(n, image_features, text_embed, image_head, logit_scale):
    rows, width = text_embed.shape
    depth, feat = image_head.shape[0], image_features.shape[1]
    pairs = n * rows
    half = width // 2
    bf16, f32 = jnp.bfloat16, jnp.float32
    vmem = pl.BlockSpec(memory_space=pltpu.VMEM)
    return pl.pallas_call(
        functools.partial(step_kernel, n),
        out_shape=(
            jax.ShapeDtypeStruct((rows, feat), bf16),
            jax.ShapeDtypeStruct((rows, width), bf16),
            jax.ShapeDtypeStruct((depth, width), f32),
        ),
        in_specs=[vmem, vmem, vmem, pl.BlockSpec(memory_space=pltpu.SMEM)],
        out_specs=(vmem, vmem, vmem),
        scratch_shapes=[
            pltpu.VMEM((n * depth, width), bf16),
            pltpu.VMEM((pairs, width), bf16),
            pltpu.VMEM((pairs, width), bf16),
            pltpu.VMEM((n, rows, depth), bf16),
            pltpu.VMEM((n, depth, rows), bf16),
            pltpu.VMEM((pairs, pairs), f32),
            pltpu.VMEM((pairs, 1), f32),
            pltpu.VMEM((1, pairs), f32),
            pltpu.VMEM((2, n - 1, depth, half), bf16),
            pltpu.VMEM((2, n - 1, depth, half), bf16),
            pltpu.SemaphoreType.DMA((4, 2, n - 1)),
            pltpu.SemaphoreType.DMA((4, 2, n - 1)),
        ],
        compiler_params=pltpu.CompilerParams(
            collective_id=0, has_side_effects=True, vmem_limit_bytes=40 * 2**20
        ),
    )(image_features, text_embed, image_head, logit_scale)


def fits_kernel(n, rows, width, depth, feat):
    pairs = n * rows
    size = 4 * pairs * pairs + 4 * pairs * width + 8 * n * depth * width + 12 * rows * feat
    return (
        n % 2 == 0
        and n >= 6
        and rows % 128 == 0
        and width % 256 == 0
        and depth % 16 == 0
        and feat == n * depth
        and size <= 24 * 2**20
    )


def solution(mesh):
    n = mesh.shape["dp"]
    groups = mesh.shape["rep"] * n

    def step(image_features, text_embed, image_head, logit_scale):
        rows, width = text_embed.shape[0] // groups, text_embed.shape[1]
        depth, feat = image_head.shape[0] // groups, image_features.shape[1]
        if fits_kernel(n, rows, width, depth, feat):
            body = functools.partial(local_kernel, n)
        else:
            body = local
        split = P(("rep", "dp"), None)
        return jax.shard_map(
            body,
            mesh=mesh,
            in_specs=(split, split, split, P()),
            out_specs=(split, split, split),
            check_vma=False,
        )(image_features, text_embed, image_head, logit_scale)

    return step
```

```python
import functools

import jax
import jax.numpy as jnp
from jax import lax
from jax.experimental import pallas as pl
from jax.experimental.pallas import tpu as pltpu
from jax.sharding import PartitionSpec as P


def unit_rows(embedding):
    inv_norm = lax.rsqrt(jnp.sum(embedding * embedding, axis=1, keepdims=True) + 1e-06)
    return (embedding * inv_norm, inv_norm)


def norm_backward(embedding, inv_norm, upstream):
    inner = jnp.sum(embedding * upstream, axis=1, keepdims=True)
    return (inv_norm * upstream - embedding * (inv_norm * inv_norm * inv_norm) * inner).astype(
        jnp.bfloat16
    )


def tile_logits(logit_mult, left_rows, right_rows):
    product = lax.dot_general(
        left_rows, right_rows, (((1,), (1,)), ((), ())), preferred_element_type=jnp.float32
    )
    return logit_mult * product


def pair_coef(logits, left_lse, right_lse, left_ids, right_ids):
    label = (left_ids[:, None] == right_ids[None, :]).astype(jnp.float32)
    values = (
        jnp.exp(logits - left_lse[:, None]) + jnp.exp(logits - right_lse[None, :]) - 2.0 * label
    )
    return values.astype(jnp.bfloat16)


def local(image_features, text_embed, image_head, logit_scale):
    logit_mult = logit_scale[0]
    row_count = image_features.shape[0]
    own_ids = lax.axis_index("dp") * row_count + jnp.arange(row_count, dtype=jnp.int32)
    head_full = lax.all_gather(image_head, "dp", axis=0, tiled=True)
    img_emb = jnp.dot(image_features, head_full, preferred_element_type=jnp.float32)
    img_scaled, img_inv = unit_rows(img_emb)
    img_unit = img_scaled.astype(jnp.bfloat16)
    txt_emb = text_embed.astype(jnp.float32)
    txt_scaled, txt_inv = unit_rows(txt_emb)
    txt_unit = txt_scaled.astype(jnp.bfloat16)
    exp_tile = jnp.exp(
        tile_logits(logit_mult, img_unit, lax.all_gather(txt_unit, "dp", axis=0, tiled=True))
    )
    col_part = jnp.sum(exp_tile, axis=0)
    row_sum, col_part = (jnp.sum(exp_tile, axis=1), col_part)
    row_lse = jnp.log(row_sum)
    col_lse = jnp.log(lax.psum_scatter(col_part, "dp", scatter_dimension=0, tiled=True))
    row_all, col_all = (
        lax.all_gather(row_lse, "dp", axis=0, tiled=True),
        lax.all_gather(col_lse, "dp", axis=0, tiled=True),
    )
    img_piece = lax.all_gather(img_unit, "dp", axis=0, tiled=True)
    txt_piece = lax.all_gather(txt_unit, "dp", axis=0, tiled=True)
    count = img_piece.shape[0]
    piece_ids = jnp.arange(count, dtype=jnp.int32)
    img_coef = pair_coef(
        tile_logits(logit_mult, img_unit, txt_piece), row_lse, col_all, own_ids, piece_ids
    )
    txt_coef = pair_coef(
        tile_logits(logit_mult, txt_unit, img_piece), col_lse, row_all, own_ids, piece_ids
    )
    img_acc = jnp.dot(img_coef, txt_piece, preferred_element_type=jnp.float32)
    txt_acc = jnp.dot(txt_coef, img_piece, preferred_element_type=jnp.float32)
    img_unit_grad = logit_mult * img_acc
    txt_unit_grad = logit_mult * txt_acc
    img_emb_grad = norm_backward(img_emb, img_inv, img_unit_grad)
    text_embed_grad = norm_backward(txt_emb, txt_inv, txt_unit_grad)
    image_features_grad = lax.dot_general(
        img_emb_grad, head_full, (((1,), (1,)), ((), ())), preferred_element_type=jnp.float32
    ).astype(jnp.bfloat16)
    head_partial = lax.dot_general(
        image_features, img_emb_grad, (((0,), (0,)), ((), ())), preferred_element_type=jnp.float32
    )
    image_head_grad = lax.psum_scatter(
        head_partial.astype(jnp.bfloat16), "dp", scatter_dimension=0, tiled=True
    ).astype(jnp.float32)
    return (image_features_grad, text_embed_grad, image_head_grad)


MESH = pl.DeviceIdType.MESH
HEAD, TEXT, IMAGE, GRAD = range(4)
ROWS_ROWS = (((1,), (1,)), ((), ()))


def place_of(index, n):
    depth, side = lax.div(index, 2), lax.rem(index, 2)
    return depth + side * (n - 1 - 2 * depth)


def index_at(place, n):
    place = lax.rem(place + 2 * n, n)
    side = lax.div(place, n // 2)
    return 2 * (place + side * (n - 1 - 2 * place)) + side


def step_kernel(
    n,
    feat_hbm,
    text_hbm,
    head_hbm,
    scale_ref,
    feat_grad_ref,
    text_grad_ref,
    head_grad_ref,
    head_all,
    text_all,
    image_all,
    feat_blocks,
    feat_t_blocks,
    feat_ref,
    text_ref,
    exp_blocks,
    stats,
    inv_cols,
    outgoing,
    incoming,
    load_sem,
    send_sem,
    recv_sem,
    stats_send_sem,
    stats_recv_sem,
):
    rows, width = text_hbm.shape
    depth = head_hbm.shape[0]
    pairs = n * rows
    half = width // 2
    messages = n - 1
    me = lax.axis_index("dp")
    place = place_of(me, n)
    partner = {+1: index_at(place + 1, n), -1: index_at(place - 1, n)}

    own_head = head_all.at[pl.ds(pl.multiple_of(me * depth, 16), depth), :]
    loads = [
        pltpu.make_async_copy(head_hbm, own_head, load_sem.at[0]),
        pltpu.make_async_copy(text_hbm, text_ref, load_sem.at[1]),
        pltpu.make_async_copy(feat_hbm, feat_ref, load_sem.at[2]),
    ]
    for load in loads:
        load.start()
    barrier = pltpu.get_barrier_semaphore()
    for k in range(1, n):
        pl.semaphore_signal(
            barrier, inc=1, device_id={"dp": lax.rem(me + k, n)}, device_id_type=MESH
        )
    loads[0].wait()
    pl.semaphore_wait(barrier, n - 1)

    def columns(way, m):
        first = (m % 2 == 0) == (way == 1)
        return pl.ds(0 if first else half, half)

    def remote(kind, way, m, src, dst):
        side = 0 if way == 1 else 1
        return pltpu.make_async_remote_copy(
            src_ref=src,
            dst_ref=dst,
            send_sem=send_sem.at[kind, side, m],
            recv_sem=recv_sem.at[kind, side, m],
            device_id={"dp": partner[way]},
            device_id_type=MESH,
        )

    gathered = {HEAD: (head_all, depth), TEXT: (text_all, rows), IMAGE: (image_all, rows)}

    def gather_copy(kind, way, m, origin_shift):
        buf, block = gathered[kind]
        owner = index_at(place - way * origin_shift, n)
        ref = buf.at[pl.ds(pl.multiple_of(owner * block, 16), block), columns(way, m)]
        return remote(kind, way, m, ref, ref)

    def gather_send(kind, m):
        for way in (1, -1):
            if m >= 2:
                gather_copy(kind, way, m - 2, m // 2).wait_recv()
            gather_copy(kind, way, m, m // 2).start()

    def gather_last(kind):
        for m in range(max(messages - 2, 0), messages):
            for way in (1, -1):
                gather_copy(kind, way, m, m // 2 + 1).wait_recv()

    gather_send(HEAD, 0)
    gather_send(HEAD, 1)

    loads[1].wait()
    txt_emb = text_ref[...].astype(jnp.float32)
    txt_scaled, txt_inv = unit_rows(txt_emb)
    text_all[pl.ds(pl.multiple_of(me * rows, 16), rows), :] = txt_scaled.astype(jnp.bfloat16)
    loads[2].wait()
    feat_t = feat_ref[...].astype(jnp.float32).T
    for b in range(n):
        block = feat_t[b * depth : (b + 1) * depth]
        feat_t_blocks[b] = block.astype(jnp.bfloat16)
        feat_blocks[b] = block.T.astype(jnp.bfloat16)

    def emb_part(owner):
        return jnp.dot(
            feat_blocks[owner],
            head_all[pl.ds(pl.multiple_of(owner * depth, 16), depth), :],
            preferred_element_type=jnp.float32,
        )

    img_emb = emb_part(me)
    for m in range(2, messages):
        gather_send(HEAD, m)
        if m % 2 == 1:
            for way in (1, -1):
                img_emb += emb_part(index_at(place - way * (m // 2), n))
    gather_send(TEXT, 0)
    gather_send(TEXT, 1)
    gather_last(HEAD)
    for way in (1, -1):
        img_emb += emb_part(index_at(place - way * (n // 2 - 1), n))
    img_emb += emb_part(index_at(place + n // 2, n))
    img_scaled, img_inv = unit_rows(img_emb)
    img_unit = img_scaled.astype(jnp.bfloat16)
    image_all[pl.ds(pl.multiple_of(me * rows, 16), rows), :] = img_unit

    scale = scale_ref[0]

    def exp_block(owner):
        at = pl.ds(pl.multiple_of(owner * rows, 16), rows)
        exp_blocks[owner] = jnp.exp(tile_logits(scale, img_unit, text_all[at, :]))

    image_sent = 0
    for m in range(2, messages):
        gather_send(TEXT, m)
        if m % 2 == 0 and image_sent < 2:
            gather_send(IMAGE, image_sent)
            image_sent += 1
        if m == 2:
            exp_block(me)
        if m % 2 == 1:
            for way in (1, -1):
                exp_block(index_at(place - way * (m // 2), n))
    gather_last(TEXT)
    for way in (1, -1):
        exp_block(index_at(place - way * (n // 2 - 1), n))
    exp_block(index_at(place + n // 2, n))

    exp_rows = jnp.concatenate([exp_blocks[b] for b in range(n)], axis=1)
    row_sum = jnp.sum(exp_rows, axis=1, keepdims=True)
    stats[me, :, 0:pairs] = jnp.sum(exp_rows, axis=0, keepdims=True)
    stats[me, :, pairs : pairs + rows] = jnp.broadcast_to(row_sum, (rows, rows)).T[0:1, :]

    def stats_copy(k, sender):
        return pltpu.make_async_remote_copy(
            src_ref=stats.at[sender],
            dst_ref=stats.at[sender],
            send_sem=stats_send_sem.at[k - 1],
            recv_sem=stats_recv_sem.at[k - 1],
            device_id={"dp": lax.rem(me + k, n)},
            device_id_type=MESH,
        )

    for k in range(1, n):
        stats_copy(k, me).start()
    while image_sent < messages - 2:
        gather_send(IMAGE, image_sent)
        image_sent += 1
    for k in range(1, n):
        stats_copy(k, lax.rem(me - k + n, n)).wait_recv()

    col_sum = stats[0, :, 0:pairs]
    for b in range(1, n):
        col_sum += stats[b, :, 0:pairs]
    inv_col = 1.0 / col_sum
    inv_cols[...] = inv_col
    row_ids = lax.broadcasted_iota(jnp.int32, (rows, pairs), 0) + me * rows
    label = (row_ids == lax.broadcasted_iota(jnp.int32, (rows, pairs), 1)).astype(jnp.float32)
    img_coef = exp_rows * (1.0 / row_sum + inv_col) - 2.0 * label
    img_acc = jnp.dot(
        img_coef.astype(jnp.bfloat16), text_all[...], preferred_element_type=jnp.float32
    )
    img_emb_grad = norm_backward(img_emb, img_inv, scale * img_acc)

    def head_part(owner, cols):
        return jnp.dot(
            feat_t_blocks[owner],
            img_emb_grad[:, cols.start : cols.start + half],
            preferred_element_type=jnp.float32,
        )

    def grad_copy(way, m):
        side = 0 if way == 1 else 1
        return remote(GRAD, way, m, outgoing.at[side, m], incoming.at[side, m])

    def grad_send(m):
        for way in (1, -1):
            side = 0 if way == 1 else 1
            value = head_part(index_at(place + way * (n // 2 - (m + 1) // 2), n), columns(way, m))
            if m >= 2:
                grad_copy(way, m - 2).wait_recv()
                value += incoming[side, m - 2].astype(jnp.float32)
            outgoing[side, m] = value.astype(jnp.bfloat16)
            grad_copy(way, m).start()

    def text_side():
        own = pl.ds(pl.multiple_of(me * rows, 128), rows)
        own_text = text_all[pl.ds(pl.multiple_of(me * rows, 16), rows), :]
        exp_texts = jnp.exp(tile_logits(scale, own_text, image_all[...]))
        inv_row = 1.0 / jnp.concatenate(
            [stats[b, :, pairs : pairs + rows] for b in range(n)], axis=1
        )
        inv_own = jnp.broadcast_to(inv_cols[:, own], (rows, rows)).T[:, 0:1]
        coef = exp_texts * (inv_own + inv_row) - 2.0 * label
        acc = jnp.dot(
            coef.astype(jnp.bfloat16), image_all[...], preferred_element_type=jnp.float32
        )
        text_grad_ref[...] = norm_backward(txt_emb, txt_inv, scale * acc)

    def feat_side():
        feat_grad_ref[...] = lax.dot_general(
            img_emb_grad, head_all[...], ROWS_ROWS, preferred_element_type=jnp.float32
        ).astype(jnp.bfloat16)

    for m in range(messages):
        grad_send(m)
        if m >= 1 and image_sent < messages:
            gather_send(IMAGE, image_sent)
            image_sent += 1
        if m == 2:
            feat_side()
        if m == messages - 2:
            gather_last(IMAGE)
            text_side()

    total = [head_part(me, pl.ds(0, half)), head_part(me, pl.ds(half, half))]
    for m in range(messages - 2, messages):
        for way in (1, -1):
            grad_copy(way, m).wait_recv()
            which = columns(way, m).start // half
            total[which] += incoming[0 if way == 1 else 1, m].astype(jnp.float32)
    head_grad_ref[:, 0:half] = total[0]
    head_grad_ref[:, half:width] = total[1]

    for m in range(messages):
        for way in (1, -1):
            for kind in gathered:
                gather_copy(kind, way, m, m // 2).wait_send()
            grad_copy(way, m).wait_send()
    for k in range(1, n):
        stats_copy(k, me).wait_send()


def local_kernel(n, image_features, text_embed, image_head, logit_scale):
    rows, width = text_embed.shape
    depth, feat = image_head.shape[0], image_features.shape[1]
    pairs = n * rows
    half = width // 2
    bf16, f32 = jnp.bfloat16, jnp.float32
    vmem = pl.BlockSpec(memory_space=pltpu.VMEM)
    hbm = pl.BlockSpec(memory_space=pltpu.HBM)
    return pl.pallas_call(
        functools.partial(step_kernel, n),
        out_shape=(
            jax.ShapeDtypeStruct((rows, feat), bf16),
            jax.ShapeDtypeStruct((rows, width), bf16),
            jax.ShapeDtypeStruct((depth, width), f32),
        ),
        in_specs=[hbm, hbm, hbm, pl.BlockSpec(memory_space=pltpu.SMEM)],
        out_specs=(vmem, vmem, vmem),
        scratch_shapes=[
            pltpu.VMEM((n * depth, width), bf16),
            pltpu.VMEM((pairs, width), bf16),
            pltpu.VMEM((pairs, width), bf16),
            pltpu.VMEM((n, rows, depth), bf16),
            pltpu.VMEM((n, depth, rows), bf16),
            pltpu.VMEM((rows, feat), bf16),
            pltpu.VMEM((rows, width), bf16),
            pltpu.VMEM((n, rows, rows), f32),
            pltpu.VMEM((n, 1, pairs + rows), f32),
            pltpu.VMEM((1, pairs), f32),
            pltpu.VMEM((2, n - 1, depth, half), bf16),
            pltpu.VMEM((2, n - 1, depth, half), bf16),
            pltpu.SemaphoreType.DMA((3,)),
            pltpu.SemaphoreType.DMA((4, 2, n - 1)),
            pltpu.SemaphoreType.DMA((4, 2, n - 1)),
            pltpu.SemaphoreType.DMA((n - 1,)),
            pltpu.SemaphoreType.DMA((n - 1,)),
        ],
        compiler_params=pltpu.CompilerParams(
            collective_id=0, has_side_effects=True, vmem_limit_bytes=62 * 2**20
        ),
    )(image_features, text_embed, image_head, logit_scale)


def fits_kernel(n, rows, width, depth, feat):
    pairs = n * rows
    size = 24 * pairs * rows + 4 * pairs * width + 8 * n * depth * width + 12 * rows * feat
    return (
        n % 2 == 0
        and n >= 6
        and rows % 128 == 0
        and width % 256 == 0
        and depth % 16 == 0
        and feat == n * depth
        and size <= 24 * 2**20
    )


def solution(mesh):
    n = mesh.shape["dp"]
    groups = mesh.shape["rep"] * n

    def step(image_features, text_embed, image_head, logit_scale):
        rows, width = text_embed.shape[0] // groups, text_embed.shape[1]
        depth, feat = image_head.shape[0] // groups, image_features.shape[1]
        if fits_kernel(n, rows, width, depth, feat):
            body = functools.partial(local_kernel, n)
        else:
            body = local
        split = P(("rep", "dp"), None)
        return jax.shard_map(
            body,
            mesh=mesh,
            in_specs=(split, split, split, P()),
            out_specs=(split, split, split),
            check_vma=False,
        )(image_features, text_embed, image_head, logit_scale)

    return step
```

```python
import functools

import jax
import jax.numpy as jnp
from jax import lax
from jax.experimental import pallas as pl
from jax.experimental.pallas import tpu as pltpu
from jax.sharding import PartitionSpec as P


def unit_rows(embedding):
    inv_norm = lax.rsqrt(jnp.sum(embedding * embedding, axis=1, keepdims=True) + 1e-06)
    return (embedding * inv_norm, inv_norm)


def norm_backward(embedding, inv_norm, upstream):
    inner = jnp.sum(embedding * upstream, axis=1, keepdims=True)
    return (inv_norm * upstream - embedding * (inv_norm * inv_norm * inv_norm) * inner).astype(
        jnp.bfloat16
    )


def tile_logits(logit_mult, left_rows, right_rows):
    product = lax.dot_general(
        left_rows, right_rows, (((1,), (1,)), ((), ())), preferred_element_type=jnp.float32
    )
    return logit_mult * product


def pair_coef(logits, left_lse, right_lse, left_ids, right_ids):
    label = (left_ids[:, None] == right_ids[None, :]).astype(jnp.float32)
    values = (
        jnp.exp(logits - left_lse[:, None]) + jnp.exp(logits - right_lse[None, :]) - 2.0 * label
    )
    return values.astype(jnp.bfloat16)


def local(image_features, text_embed, image_head, logit_scale):
    logit_mult = logit_scale[0]
    row_count = image_features.shape[0]
    own_ids = lax.axis_index("dp") * row_count + jnp.arange(row_count, dtype=jnp.int32)
    head_full = lax.all_gather(image_head, "dp", axis=0, tiled=True)
    img_emb = jnp.dot(image_features, head_full, preferred_element_type=jnp.float32)
    img_scaled, img_inv = unit_rows(img_emb)
    img_unit = img_scaled.astype(jnp.bfloat16)
    txt_emb = text_embed.astype(jnp.float32)
    txt_scaled, txt_inv = unit_rows(txt_emb)
    txt_unit = txt_scaled.astype(jnp.bfloat16)
    exp_tile = jnp.exp(
        tile_logits(logit_mult, img_unit, lax.all_gather(txt_unit, "dp", axis=0, tiled=True))
    )
    col_part = jnp.sum(exp_tile, axis=0)
    row_sum, col_part = (jnp.sum(exp_tile, axis=1), col_part)
    row_lse = jnp.log(row_sum)
    col_lse = jnp.log(lax.psum_scatter(col_part, "dp", scatter_dimension=0, tiled=True))
    row_all, col_all = (
        lax.all_gather(row_lse, "dp", axis=0, tiled=True),
        lax.all_gather(col_lse, "dp", axis=0, tiled=True),
    )
    img_piece = lax.all_gather(img_unit, "dp", axis=0, tiled=True)
    txt_piece = lax.all_gather(txt_unit, "dp", axis=0, tiled=True)
    count = img_piece.shape[0]
    piece_ids = jnp.arange(count, dtype=jnp.int32)
    img_coef = pair_coef(
        tile_logits(logit_mult, img_unit, txt_piece), row_lse, col_all, own_ids, piece_ids
    )
    txt_coef = pair_coef(
        tile_logits(logit_mult, txt_unit, img_piece), col_lse, row_all, own_ids, piece_ids
    )
    img_acc = jnp.dot(img_coef, txt_piece, preferred_element_type=jnp.float32)
    txt_acc = jnp.dot(txt_coef, img_piece, preferred_element_type=jnp.float32)
    img_unit_grad = logit_mult * img_acc
    txt_unit_grad = logit_mult * txt_acc
    img_emb_grad = norm_backward(img_emb, img_inv, img_unit_grad)
    text_embed_grad = norm_backward(txt_emb, txt_inv, txt_unit_grad)
    image_features_grad = lax.dot_general(
        img_emb_grad, head_full, (((1,), (1,)), ((), ())), preferred_element_type=jnp.float32
    ).astype(jnp.bfloat16)
    head_partial = lax.dot_general(
        image_features, img_emb_grad, (((0,), (0,)), ((), ())), preferred_element_type=jnp.float32
    )
    image_head_grad = lax.psum_scatter(
        head_partial.astype(jnp.bfloat16), "dp", scatter_dimension=0, tiled=True
    ).astype(jnp.float32)
    return (image_features_grad, text_embed_grad, image_head_grad)


MESH = pl.DeviceIdType.MESH
HEAD, TEXT, IMAGE, GRAD = range(4)
ROWS_ROWS = (((1,), (1,)), ((), ()))


def place_of(index, n):
    depth, side = lax.div(index, 2), lax.rem(index, 2)
    return depth + side * (n - 1 - 2 * depth)


def index_at(place, n):
    place = lax.rem(place + 2 * n, n)
    side = lax.div(place, n // 2)
    return 2 * (place + side * (n - 1 - 2 * place)) + side


def step_kernel(
    n,
    feat_hbm,
    text_hbm,
    head_hbm,
    scale_ref,
    feat_out,
    text_out,
    head_out,
    feat_grad_ref,
    text_grad_ref,
    head_grad_ref,
    head_all,
    text_all,
    image_all,
    feat_blocks,
    feat_t_blocks,
    feat_ref,
    text_ref,
    exp_blocks,
    stats,
    inv_cols,
    outgoing,
    incoming,
    load_sem,
    store_sem,
    send_sem,
    recv_sem,
    stats_send_sem,
    stats_recv_sem,
):
    rows, width = text_hbm.shape
    depth = head_hbm.shape[0]
    pairs = n * rows
    half = width // 2
    messages = n - 1
    me = lax.axis_index("dp")
    place = place_of(me, n)
    partner = {+1: index_at(place + 1, n), -1: index_at(place - 1, n)}

    own_head = head_all.at[pl.ds(pl.multiple_of(me * depth, 16), depth), :]
    loads = [
        pltpu.make_async_copy(head_hbm, own_head, load_sem.at[0]),
        pltpu.make_async_copy(text_hbm, text_ref, load_sem.at[1]),
        pltpu.make_async_copy(feat_hbm, feat_ref, load_sem.at[2]),
    ]
    stores = [
        pltpu.make_async_copy(feat_grad_ref, feat_out, store_sem.at[0]),
        pltpu.make_async_copy(text_grad_ref, text_out, store_sem.at[1]),
        pltpu.make_async_copy(head_grad_ref, head_out, store_sem.at[2]),
    ]
    for load in loads:
        load.start()
    barrier = pltpu.get_barrier_semaphore()
    for k in range(1, n):
        pl.semaphore_signal(
            barrier, inc=1, device_id={"dp": lax.rem(me + k, n)}, device_id_type=MESH
        )
    loads[0].wait()
    pl.semaphore_wait(barrier, n - 1)

    def columns(way, m):
        first = (m % 2 == 0) == (way == 1)
        return pl.ds(0 if first else half, half)

    def remote(kind, way, m, src, dst):
        side = 0 if way == 1 else 1
        return pltpu.make_async_remote_copy(
            src_ref=src,
            dst_ref=dst,
            send_sem=send_sem.at[kind, side, m],
            recv_sem=recv_sem.at[kind, side, m],
            device_id={"dp": partner[way]},
            device_id_type=MESH,
        )

    gathered = {HEAD: (head_all, depth), TEXT: (text_all, rows), IMAGE: (image_all, rows)}

    def gather_copy(kind, way, m, origin_shift):
        buf, block = gathered[kind]
        owner = index_at(place - way * origin_shift, n)
        ref = buf.at[pl.ds(pl.multiple_of(owner * block, 16), block), columns(way, m)]
        return remote(kind, way, m, ref, ref)

    def gather_send(kind, m):
        for way in (1, -1):
            if m >= 2:
                gather_copy(kind, way, m - 2, m // 2).wait_recv()
            gather_copy(kind, way, m, m // 2).start()

    def gather_last(kind):
        for m in range(max(messages - 2, 0), messages):
            for way in (1, -1):
                gather_copy(kind, way, m, m // 2 + 1).wait_recv()

    gather_send(HEAD, 0)
    gather_send(HEAD, 1)

    loads[1].wait()
    txt_emb = text_ref[...].astype(jnp.float32)
    txt_scaled, txt_inv = unit_rows(txt_emb)
    text_all[pl.ds(pl.multiple_of(me * rows, 16), rows), :] = txt_scaled.astype(jnp.bfloat16)
    loads[2].wait()
    feat_t = feat_ref[...].astype(jnp.float32).T
    for b in range(n):
        block = feat_t[b * depth : (b + 1) * depth]
        feat_t_blocks[b] = block.astype(jnp.bfloat16)
        feat_blocks[b] = block.T.astype(jnp.bfloat16)

    def emb_part(owner):
        return jnp.dot(
            feat_blocks[owner],
            head_all[pl.ds(pl.multiple_of(owner * depth, 16), depth), :],
            preferred_element_type=jnp.float32,
        )

    img_emb = emb_part(me)
    for m in range(2, messages):
        gather_send(HEAD, m)
        if m % 2 == 1:
            for way in (1, -1):
                img_emb += emb_part(index_at(place - way * (m // 2), n))
    gather_send(TEXT, 0)
    gather_send(TEXT, 1)
    gather_last(HEAD)
    for way in (1, -1):
        img_emb += emb_part(index_at(place - way * (n // 2 - 1), n))
    img_emb += emb_part(index_at(place + n // 2, n))
    img_scaled, img_inv = unit_rows(img_emb)
    img_unit = img_scaled.astype(jnp.bfloat16)
    image_all[pl.ds(pl.multiple_of(me * rows, 16), rows), :] = img_unit

    scale = scale_ref[0]

    def exp_block(owner):
        at = pl.ds(pl.multiple_of(owner * rows, 16), rows)
        exp_blocks[owner] = jnp.exp(tile_logits(scale, img_unit, text_all[at, :]))

    image_sent = 0
    for m in range(2, messages):
        gather_send(TEXT, m)
        if m % 2 == 0 and image_sent < 2:
            gather_send(IMAGE, image_sent)
            image_sent += 1
        if m == 2:
            exp_block(me)
        if m % 2 == 1:
            for way in (1, -1):
                exp_block(index_at(place - way * (m // 2), n))
    gather_last(TEXT)
    for way in (1, -1):
        exp_block(index_at(place - way * (n // 2 - 1), n))
    exp_block(index_at(place + n // 2, n))

    exp_rows = jnp.concatenate([exp_blocks[b] for b in range(n)], axis=1)
    row_sum = jnp.sum(exp_rows, axis=1, keepdims=True)
    stats[me, :, 0:pairs] = jnp.sum(exp_rows, axis=0, keepdims=True)
    stats[me, :, pairs : pairs + rows] = jnp.broadcast_to(row_sum, (rows, rows)).T[0:1, :]

    def stats_copy(k, sender):
        return pltpu.make_async_remote_copy(
            src_ref=stats.at[sender],
            dst_ref=stats.at[sender],
            send_sem=stats_send_sem.at[k - 1],
            recv_sem=stats_recv_sem.at[k - 1],
            device_id={"dp": lax.rem(me + k, n)},
            device_id_type=MESH,
        )

    for k in range(1, n):
        stats_copy(k, me).start()
    while image_sent < messages - 2:
        gather_send(IMAGE, image_sent)
        image_sent += 1
    for k in range(1, n):
        stats_copy(k, lax.rem(me - k + n, n)).wait_recv()

    col_sum = stats[0, :, 0:pairs]
    for b in range(1, n):
        col_sum += stats[b, :, 0:pairs]
    inv_col = 1.0 / col_sum
    inv_cols[...] = inv_col
    row_ids = lax.broadcasted_iota(jnp.int32, (rows, pairs), 0) + me * rows
    label = (row_ids == lax.broadcasted_iota(jnp.int32, (rows, pairs), 1)).astype(jnp.float32)
    img_coef = exp_rows * (1.0 / row_sum + inv_col) - 2.0 * label
    img_acc = jnp.dot(
        img_coef.astype(jnp.bfloat16), text_all[...], preferred_element_type=jnp.float32
    )
    img_emb_grad = norm_backward(img_emb, img_inv, scale * img_acc)

    def head_part(owner, cols):
        return jnp.dot(
            feat_t_blocks[owner],
            img_emb_grad[:, cols.start : cols.start + half],
            preferred_element_type=jnp.float32,
        )

    def grad_copy(way, m):
        side = 0 if way == 1 else 1
        return remote(GRAD, way, m, outgoing.at[side, m], incoming.at[side, m])

    def grad_send(m):
        for way in (1, -1):
            side = 0 if way == 1 else 1
            value = head_part(index_at(place + way * (n // 2 - (m + 1) // 2), n), columns(way, m))
            if m >= 2:
                grad_copy(way, m - 2).wait_recv()
                value += incoming[side, m - 2].astype(jnp.float32)
            outgoing[side, m] = value.astype(jnp.bfloat16)
            grad_copy(way, m).start()

    def text_side():
        own = pl.ds(pl.multiple_of(me * rows, 128), rows)
        own_text = text_all[pl.ds(pl.multiple_of(me * rows, 16), rows), :]
        exp_texts = jnp.exp(tile_logits(scale, own_text, image_all[...]))
        inv_row = 1.0 / jnp.concatenate(
            [stats[b, :, pairs : pairs + rows] for b in range(n)], axis=1
        )
        inv_own = jnp.broadcast_to(inv_cols[:, own], (rows, rows)).T[:, 0:1]
        coef = exp_texts * (inv_own + inv_row) - 2.0 * label
        acc = jnp.dot(
            coef.astype(jnp.bfloat16), image_all[...], preferred_element_type=jnp.float32
        )
        text_grad_ref[...] = norm_backward(txt_emb, txt_inv, scale * acc)
        stores[1].start()

    def feat_side():
        feat_grad_ref[...] = lax.dot_general(
            img_emb_grad, head_all[...], ROWS_ROWS, preferred_element_type=jnp.float32
        ).astype(jnp.bfloat16)
        stores[0].start()

    for m in range(messages):
        grad_send(m)
        if m >= 1 and image_sent < messages:
            gather_send(IMAGE, image_sent)
            image_sent += 1
        if m == 2:
            feat_side()
        if m == messages - 2:
            gather_last(IMAGE)
            text_side()

    total = [head_part(me, pl.ds(0, half)), head_part(me, pl.ds(half, half))]
    for m in range(messages - 2, messages):
        for way in (1, -1):
            grad_copy(way, m).wait_recv()
            which = columns(way, m).start // half
            total[which] += incoming[0 if way == 1 else 1, m].astype(jnp.float32)
    head_grad_ref[:, 0:half] = total[0]
    head_grad_ref[:, half:width] = total[1]
    stores[2].start()

    for m in range(messages):
        for way in (1, -1):
            for kind in gathered:
                gather_copy(kind, way, m, m // 2).wait_send()
            grad_copy(way, m).wait_send()
    for k in range(1, n):
        stats_copy(k, me).wait_send()
    for store in stores:
        store.wait()


def hand_on_kernel(*refs):
    sources, results, sem = refs[:3], refs[3:6], refs[6]
    copies = [
        pltpu.make_async_copy(source, result, sem.at[i])
        for i, (source, result) in enumerate(zip(sources, results))
    ]
    for copy in copies:
        copy.start()
    for copy in copies:
        copy.wait()


def local_kernel(n, image_features, text_embed, image_head, logit_scale):
    rows, width = text_embed.shape
    depth, feat = image_head.shape[0], image_features.shape[1]
    pairs = n * rows
    half = width // 2
    bf16, f32 = jnp.bfloat16, jnp.float32
    hbm = pl.BlockSpec(memory_space=pltpu.HBM)
    out_shape = (
        jax.ShapeDtypeStruct((rows, feat), bf16),
        jax.ShapeDtypeStruct((rows, width), bf16),
        jax.ShapeDtypeStruct((depth, width), f32),
    )
    results = pl.pallas_call(
        functools.partial(step_kernel, n),
        out_shape=out_shape,
        in_specs=[hbm, hbm, hbm, pl.BlockSpec(memory_space=pltpu.SMEM)],
        out_specs=(hbm, hbm, hbm),
        scratch_shapes=[
            pltpu.VMEM((rows, feat), bf16),
            pltpu.VMEM((rows, width), bf16),
            pltpu.VMEM((depth, width), f32),
            pltpu.VMEM((n * depth, width), bf16),
            pltpu.VMEM((pairs, width), bf16),
            pltpu.VMEM((pairs, width), bf16),
            pltpu.VMEM((n, rows, depth), bf16),
            pltpu.VMEM((n, depth, rows), bf16),
            pltpu.VMEM((rows, feat), bf16),
            pltpu.VMEM((rows, width), bf16),
            pltpu.VMEM((n, rows, rows), f32),
            pltpu.VMEM((n, 1, pairs + rows), f32),
            pltpu.VMEM((1, pairs), f32),
            pltpu.VMEM((2, n - 1, depth, half), bf16),
            pltpu.VMEM((2, n - 1, depth, half), bf16),
            pltpu.SemaphoreType.DMA((3,)),
            pltpu.SemaphoreType.DMA((3,)),
            pltpu.SemaphoreType.DMA((4, 2, n - 1)),
            pltpu.SemaphoreType.DMA((4, 2, n - 1)),
            pltpu.SemaphoreType.DMA((n - 1,)),
            pltpu.SemaphoreType.DMA((n - 1,)),
        ],
        compiler_params=pltpu.CompilerParams(
            collective_id=0, has_side_effects=True, vmem_limit_bytes=62 * 2**20
        ),
    )(image_features, text_embed, image_head, logit_scale)
    return pl.pallas_call(
        hand_on_kernel,
        out_shape=out_shape,
        in_specs=[hbm, hbm, hbm],
        out_specs=(hbm, hbm, hbm),
        scratch_shapes=[pltpu.SemaphoreType.DMA((3,))],
        compiler_params=pltpu.CompilerParams(vmem_limit_bytes=62 * 2**20),
    )(*results)


def fits_kernel(n, rows, width, depth, feat):
    pairs = n * rows
    size = 24 * pairs * rows + 4 * pairs * width + 8 * n * depth * width + 12 * rows * feat
    return (
        n % 2 == 0
        and n >= 6
        and rows % 128 == 0
        and width % 256 == 0
        and depth % 16 == 0
        and feat == n * depth
        and size <= 24 * 2**20
    )


def solution(mesh):
    n = mesh.shape["dp"]
    groups = mesh.shape["rep"] * n

    def step(image_features, text_embed, image_head, logit_scale):
        rows, width = text_embed.shape[0] // groups, text_embed.shape[1]
        depth, feat = image_head.shape[0] // groups, image_features.shape[1]
        if fits_kernel(n, rows, width, depth, feat):
            body = functools.partial(local_kernel, n)
        else:
            body = local
        split = P(("rep", "dp"), None)
        return jax.shard_map(
            body,
            mesh=mesh,
            in_specs=(split, split, split, P()),
            out_specs=(split, split, split),
            check_vma=False,
        )(image_features, text_embed, image_head, logit_scale)

    return step
```

```python
import functools

import jax
import jax.numpy as jnp
from jax import lax
from jax.experimental import pallas as pl
from jax.experimental.pallas import tpu as pltpu
from jax.sharding import PartitionSpec as P


def unit_rows(embedding):
    inv_norm = lax.rsqrt(jnp.sum(embedding * embedding, axis=1, keepdims=True) + 1e-06)
    return (embedding * inv_norm, inv_norm)


def norm_backward(embedding, inv_norm, upstream):
    inner = jnp.sum(embedding * upstream, axis=1, keepdims=True)
    return (inv_norm * upstream - embedding * (inv_norm * inv_norm * inv_norm) * inner).astype(
        jnp.bfloat16
    )


def tile_logits(logit_mult, left_rows, right_rows):
    product = lax.dot_general(
        left_rows, right_rows, (((1,), (1,)), ((), ())), preferred_element_type=jnp.float32
    )
    return logit_mult * product


def pair_coef(logits, left_lse, right_lse, left_ids, right_ids):
    label = (left_ids[:, None] == right_ids[None, :]).astype(jnp.float32)
    values = (
        jnp.exp(logits - left_lse[:, None]) + jnp.exp(logits - right_lse[None, :]) - 2.0 * label
    )
    return values.astype(jnp.bfloat16)


def local(image_features, text_embed, image_head, logit_scale):
    logit_mult = logit_scale[0]
    row_count = image_features.shape[0]
    own_ids = lax.axis_index("dp") * row_count + jnp.arange(row_count, dtype=jnp.int32)
    head_full = lax.all_gather(image_head, "dp", axis=0, tiled=True)
    img_emb = jnp.dot(image_features, head_full, preferred_element_type=jnp.float32)
    img_scaled, img_inv = unit_rows(img_emb)
    img_unit = img_scaled.astype(jnp.bfloat16)
    txt_emb = text_embed.astype(jnp.float32)
    txt_scaled, txt_inv = unit_rows(txt_emb)
    txt_unit = txt_scaled.astype(jnp.bfloat16)
    exp_tile = jnp.exp(
        tile_logits(logit_mult, img_unit, lax.all_gather(txt_unit, "dp", axis=0, tiled=True))
    )
    col_part = jnp.sum(exp_tile, axis=0)
    row_sum, col_part = (jnp.sum(exp_tile, axis=1), col_part)
    row_lse = jnp.log(row_sum)
    col_lse = jnp.log(lax.psum_scatter(col_part, "dp", scatter_dimension=0, tiled=True))
    row_all, col_all = (
        lax.all_gather(row_lse, "dp", axis=0, tiled=True),
        lax.all_gather(col_lse, "dp", axis=0, tiled=True),
    )
    img_piece = lax.all_gather(img_unit, "dp", axis=0, tiled=True)
    txt_piece = lax.all_gather(txt_unit, "dp", axis=0, tiled=True)
    count = img_piece.shape[0]
    piece_ids = jnp.arange(count, dtype=jnp.int32)
    img_coef = pair_coef(
        tile_logits(logit_mult, img_unit, txt_piece), row_lse, col_all, own_ids, piece_ids
    )
    txt_coef = pair_coef(
        tile_logits(logit_mult, txt_unit, img_piece), col_lse, row_all, own_ids, piece_ids
    )
    img_acc = jnp.dot(img_coef, txt_piece, preferred_element_type=jnp.float32)
    txt_acc = jnp.dot(txt_coef, img_piece, preferred_element_type=jnp.float32)
    img_unit_grad = logit_mult * img_acc
    txt_unit_grad = logit_mult * txt_acc
    img_emb_grad = norm_backward(img_emb, img_inv, img_unit_grad)
    text_embed_grad = norm_backward(txt_emb, txt_inv, txt_unit_grad)
    image_features_grad = lax.dot_general(
        img_emb_grad, head_full, (((1,), (1,)), ((), ())), preferred_element_type=jnp.float32
    ).astype(jnp.bfloat16)
    head_partial = lax.dot_general(
        image_features, img_emb_grad, (((0,), (0,)), ((), ())), preferred_element_type=jnp.float32
    )
    image_head_grad = lax.psum_scatter(
        head_partial.astype(jnp.bfloat16), "dp", scatter_dimension=0, tiled=True
    ).astype(jnp.float32)
    return (image_features_grad, text_embed_grad, image_head_grad)


MESH = pl.DeviceIdType.MESH
HEAD, GRAD = range(2)
IMAGES, IMAGE_GRADS, ROW_SUMS = range(3)
ROWS_ROWS = (((1,), (1,)), ((), ()))
COLS_COLS = (((0,), (0,)), ((), ()))


def place_of(index, n):
    depth, side = lax.div(index, 2), lax.rem(index, 2)
    return depth + side * (n - 1 - 2 * depth)


def index_at(place, n):
    place = lax.rem(place + 2 * n, n)
    side = lax.div(place, n // 2)
    return 2 * (place + side * (n - 1 - 2 * place)) + side


def step_kernel(
    n,
    feat_hbm,
    text_hbm,
    head_hbm,
    scale_ref,
    feat_out,
    text_out,
    head_out,
    feat_grad_ref,
    text_grad_ref,
    head_grad_ref,
    head_all,
    text_col,
    images,
    feat_blocks,
    feat_t_blocks,
    feat_ref,
    text_ref,
    coefs,
    row_stats,
    col_stats,
    image_out,
    image_in,
    text_part,
    text_going,
    text_coming,
    outgoing,
    incoming,
    load_sem,
    store_sem,
    send_sem,
    recv_sem,
    pair_send_sem,
    pair_recv_sem,
    stats_send_sem,
    stats_recv_sem,
    chain_send_sem,
    chain_recv_sem,
):
    rows, width = text_hbm.shape
    depth = head_hbm.shape[0]
    half = width // 2
    length = n // 2
    messages = n - 1
    me = lax.axis_index("dp")
    place = place_of(me, n)
    level, side = lax.div(me, 2), lax.rem(me, 2)
    other = me + 1 - 2 * side
    partner = {+1: index_at(place + 1, n), -1: index_at(place - 1, n)}

    own_head = head_all.at[pl.ds(pl.multiple_of(me * depth, 16), depth), :]
    loads = [
        pltpu.make_async_copy(head_hbm, own_head, load_sem.at[0]),
        pltpu.make_async_copy(text_hbm, text_ref, load_sem.at[1]),
        pltpu.make_async_copy(feat_hbm, feat_ref, load_sem.at[2]),
    ]
    stores = [
        pltpu.make_async_copy(feat_grad_ref, feat_out, store_sem.at[0]),
        pltpu.make_async_copy(text_grad_ref, text_out, store_sem.at[1]),
        pltpu.make_async_copy(head_grad_ref, head_out, store_sem.at[2]),
    ]
    for load in loads:
        load.start()
    barrier = pltpu.get_barrier_semaphore()
    for k in range(1, n):
        pl.semaphore_signal(
            barrier, inc=1, device_id={"dp": lax.rem(me + k, n)}, device_id_type=MESH
        )
    loads[0].wait()
    pl.semaphore_wait(barrier, n - 1)

    def columns(way, m):
        first = (m % 2 == 0) == (way == 1)
        return pl.ds(0 if first else half, half)

    def remote(kind, way, m, src, dst):
        side = 0 if way == 1 else 1
        return pltpu.make_async_remote_copy(
            src_ref=src,
            dst_ref=dst,
            send_sem=send_sem.at[kind, side, m],
            recv_sem=recv_sem.at[kind, side, m],
            device_id={"dp": partner[way]},
            device_id_type=MESH,
        )

    gathered = {HEAD: (head_all, depth)}

    def gather_copy(kind, way, m, origin_shift):
        buf, block = gathered[kind]
        owner = index_at(place - way * origin_shift, n)
        ref = buf.at[pl.ds(pl.multiple_of(owner * block, 16), block), columns(way, m)]
        return remote(kind, way, m, ref, ref)

    def gather_send(kind, m):
        for way in (1, -1):
            if m >= 2:
                gather_copy(kind, way, m - 2, m // 2).wait_recv()
            gather_copy(kind, way, m, m // 2).start()

    def gather_last(kind):
        for m in range(max(messages - 2, 0), messages):
            for way in (1, -1):
                gather_copy(kind, way, m, m // 2 + 1).wait_recv()

    def along(way):
        return level if way == 1 else length - 1 - level

    def chain_copy(kind, way, slot, src, dst):
        return pltpu.make_async_remote_copy(
            src_ref=src,
            dst_ref=dst,
            send_sem=chain_send_sem.at[kind, 0 if way == 1 else 1, slot],
            recv_sem=chain_recv_sem.at[kind, 0 if way == 1 else 1, slot],
            device_id={"dp": lax.rem(me + 2 * way + n, n)},
            device_id_type=MESH,
        )

    def text_copy(way, slot, shift):
        owner = level - way * shift
        ref = text_col.at[pl.ds(pl.multiple_of(owner * rows, 16), rows), :]
        return chain_copy(0, way, slot, ref, ref)

    def text_slot(slot):
        for way in (1, -1):
            if slot >= 1:

                @pl.when(along(way) >= slot)
                def _():
                    text_copy(way, slot - 1, slot).wait_recv()

            if slot <= length - 2:

                @pl.when((along(way) >= slot) & (along(way) < length - 1))
                def _():
                    text_copy(way, slot, slot).start()

    def pair_copy(kind, src, dst):
        return pltpu.make_async_remote_copy(
            src_ref=src,
            dst_ref=dst,
            send_sem=pair_send_sem.at[kind],
            recv_sem=pair_recv_sem.at[kind],
            device_id={"dp": other},
            device_id_type=MESH,
        )

    own_images = pl.ds(pl.multiple_of(side * rows, 16), rows)
    other_images = pl.ds(pl.multiple_of((1 - side) * rows, 16), rows)
    images_copy = pair_copy(IMAGES, images.at[own_images, :], images.at[own_images, :])
    images_landed = pair_copy(IMAGES, images.at[other_images, :], images.at[other_images, :])
    grads_copy = pair_copy(IMAGE_GRADS, image_out, image_in)
    sums_copy = pair_copy(ROW_SUMS, row_stats.at[side], row_stats.at[side])
    sums_landed = pair_copy(ROW_SUMS, row_stats.at[1 - side], row_stats.at[1 - side])

    gather_send(HEAD, 0)
    gather_send(HEAD, 1)

    loads[1].wait()
    txt_emb = text_ref[...].astype(jnp.float32)
    txt_scaled, txt_inv = unit_rows(txt_emb)
    text_col[pl.ds(pl.multiple_of(level * rows, 16), rows), :] = txt_scaled.astype(jnp.bfloat16)
    loads[2].wait()
    feat_t = feat_ref[...].astype(jnp.float32).T
    for b in range(n):
        block = feat_t[b * depth : (b + 1) * depth]
        feat_t_blocks[b] = block.astype(jnp.bfloat16)
        feat_blocks[b] = block.T.astype(jnp.bfloat16)

    def emb_part(owner):
        return jnp.dot(
            feat_blocks[owner],
            head_all[pl.ds(pl.multiple_of(owner * depth, 16), depth), :],
            preferred_element_type=jnp.float32,
        )

    img_emb = emb_part(me)
    for m in range(2, messages):
        gather_send(HEAD, m)
        if m % 2 == 1:
            for way in (1, -1):
                img_emb += emb_part(index_at(place - way * (m // 2), n))
        if m == messages - 2:
            text_slot(0)
    gather_last(HEAD)
    text_slot(1)
    for way in (1, -1):
        img_emb += emb_part(index_at(place - way * (n // 2 - 1), n))
    img_emb += emb_part(index_at(place + n // 2, n))
    img_scaled, img_inv = unit_rows(img_emb)
    img_unit = img_scaled.astype(jnp.bfloat16)
    images[own_images, :] = img_unit
    images_copy.start()
    for slot in range(2, length):
        text_slot(slot)

    scale = scale_ref[0]
    images_landed.wait_recv()
    exp_tile = jnp.exp(tile_logits(scale, images[...], text_col[...]))
    row_part = jnp.sum(exp_tile, axis=1, keepdims=True)
    row_stats[side] = jnp.broadcast_to(row_part, (2 * rows, rows)).T[0:1, :]
    col_stats[level] = jnp.sum(exp_tile, axis=0, keepdims=True)

    def stats_copy(k, sender):
        return pltpu.make_async_remote_copy(
            src_ref=col_stats.at[sender],
            dst_ref=col_stats.at[sender],
            send_sem=stats_send_sem.at[k - 1],
            recv_sem=stats_recv_sem.at[k - 1],
            device_id={"dp": 2 * lax.rem(level + k, length) + side},
            device_id_type=MESH,
        )

    for k in range(1, length):
        stats_copy(k, level).start()
    sums_copy.start()
    sums_landed.wait_recv()
    inv_row = 1.0 / jnp.broadcast_to(row_stats[0] + row_stats[1], (rows, 2 * rows)).T[:, 0:1]
    tile = (2 * rows, length * rows)
    row_ids = lax.broadcasted_iota(jnp.int32, tile, 0) - side * rows
    col_ids = lax.broadcasted_iota(jnp.int32, tile, 1) - level * rows
    label = (row_ids == col_ids) & (row_ids >= 0) & (row_ids < rows)
    minus = jnp.where(label, 2.0, 0.0)
    for k in range(1, length):
        stats_copy(k, lax.rem(level - k + length, length)).wait_recv()
    col_sum = col_stats[0]
    for k in range(1, length):
        col_sum += col_stats[k]
    coefs[...] = (exp_tile * (inv_row + 1.0 / col_sum) - minus).astype(jnp.bfloat16)

    image_out[...] = jnp.dot(
        coefs[other_images, :], text_col[...], preferred_element_type=jnp.float32
    ).astype(jnp.bfloat16)
    grads_copy.start()
    text_acc = lax.dot_general(
        coefs[...], images[...], COLS_COLS, preferred_element_type=jnp.float32
    )
    for b in range(length):
        text_part[b] = text_acc[b * rows : (b + 1) * rows]

    def text_grad_copy(way, slot):
        which = 0 if way == 1 else 1
        return chain_copy(1, way, slot, text_going.at[which, slot], text_coming.at[which, slot])

    def text_grad_slot(slot):
        for way in (1, -1):
            which = 0 if way == 1 else 1

            @pl.when(along(way) <= slot)
            def _():
                ahead = length - 1 - slot + along(way)
                value = text_part[ahead if way == 1 else length - 1 - ahead]
                text_going[which, slot] = value.astype(jnp.bfloat16)

            if slot >= 1:

                @pl.when((along(way) <= slot) & (along(way) >= 1))
                def _():
                    ahead = length - 1 - slot + along(way)
                    value = text_part[ahead if way == 1 else length - 1 - ahead]
                    text_grad_copy(way, slot - 1).wait_recv()
                    value += text_coming[which, slot - 1].astype(jnp.float32)
                    text_going[which, slot] = value.astype(jnp.bfloat16)

            @pl.when(along(way) <= slot)
            def _():
                text_grad_copy(way, slot).start()

    text_grad_slot(0)
    img_acc = jnp.dot(
        coefs[own_images, :], text_col[...], preferred_element_type=jnp.float32
    )
    grads_copy.wait_recv()
    img_acc += image_in[...].astype(jnp.float32)
    img_emb_grad = norm_backward(img_emb, img_inv, scale * img_acc)

    def head_part(owner, cols):
        return jnp.dot(
            feat_t_blocks[owner],
            img_emb_grad[:, cols.start : cols.start + half],
            preferred_element_type=jnp.float32,
        )

    def grad_copy(way, m):
        side = 0 if way == 1 else 1
        return remote(GRAD, way, m, outgoing.at[side, m], incoming.at[side, m])

    def grad_send(m):
        for way in (1, -1):
            side = 0 if way == 1 else 1
            value = head_part(index_at(place + way * (n // 2 - (m + 1) // 2), n), columns(way, m))
            if m >= 2:
                grad_copy(way, m - 2).wait_recv()
                value += incoming[side, m - 2].astype(jnp.float32)
            outgoing[side, m] = value.astype(jnp.bfloat16)
            grad_copy(way, m).start()

    def text_side():
        for way in (1, -1):
            which = 0 if way == 1 else 1

            @pl.when(along(way) >= 1)
            def _():
                text_grad_copy(way, length - 2).wait_recv()
                text_part[level] += text_coming[which, length - 2].astype(jnp.float32)

        text_grad_ref[...] = norm_backward(txt_emb, txt_inv, scale * text_part[level])
        stores[1].start()

    def feat_side():
        feat_grad_ref[...] = lax.dot_general(
            img_emb_grad, head_all[...], ROWS_ROWS, preferred_element_type=jnp.float32
        ).astype(jnp.bfloat16)
        stores[0].start()

    for m in range(messages):
        grad_send(m)
        if m >= 1 and m <= length - 2:
            text_grad_slot(m)
        if m == length - 1:
            feat_side()
        if m == messages - 2:
            text_side()

    total = [head_part(me, pl.ds(0, half)), head_part(me, pl.ds(half, half))]
    for m in range(messages - 2, messages):
        for way in (1, -1):
            grad_copy(way, m).wait_recv()
            which = columns(way, m).start // half
            total[which] += incoming[0 if way == 1 else 1, m].astype(jnp.float32)
    head_grad_ref[:, 0:half] = total[0]
    head_grad_ref[:, half:width] = total[1]
    stores[2].start()

    for m in range(messages):
        for way in (1, -1):
            for kind in gathered:
                gather_copy(kind, way, m, m // 2).wait_send()
            grad_copy(way, m).wait_send()
    for k in range(1, length):
        stats_copy(k, level).wait_send()
    images_copy.wait_send()
    grads_copy.wait_send()
    sums_copy.wait_send()
    for way in (1, -1):
        for slot in range(length - 1):

            @pl.when((along(way) >= slot) & (along(way) < length - 1))
            def _():
                text_copy(way, slot, slot).wait_send()

            @pl.when(along(way) <= slot)
            def _():
                text_grad_copy(way, slot).wait_send()

    for store in stores:
        store.wait()


def hand_on_kernel(*refs):
    sources, results, held, sem = refs[:3], refs[3:6], refs[6:9], refs[9]
    loads = [pltpu.make_async_copy(sources[i], held[i], sem.at[0, i]) for i in range(3)]
    stores = [pltpu.make_async_copy(held[i], results[i], sem.at[1, i]) for i in range(3)]
    for load in loads:
        load.start()
    for load, store in zip(loads, stores):
        load.wait()
        store.start()
    for store in stores:
        store.wait()


def local_kernel(n, image_features, text_embed, image_head, logit_scale):
    rows, width = text_embed.shape
    depth, feat = image_head.shape[0], image_features.shape[1]
    length = n // 2
    half = width // 2
    bf16, f32 = jnp.bfloat16, jnp.float32
    hbm = pl.BlockSpec(memory_space=pltpu.HBM)
    out_shape = (
        jax.ShapeDtypeStruct((rows, feat), bf16),
        jax.ShapeDtypeStruct((rows, width), bf16),
        jax.ShapeDtypeStruct((depth, width), f32),
    )
    results = pl.pallas_call(
        functools.partial(step_kernel, n),
        out_shape=out_shape,
        in_specs=[hbm, hbm, hbm, pl.BlockSpec(memory_space=pltpu.SMEM)],
        out_specs=(hbm, hbm, hbm),
        scratch_shapes=[
            pltpu.VMEM((rows, feat), bf16),
            pltpu.VMEM((rows, width), bf16),
            pltpu.VMEM((depth, width), f32),
            pltpu.VMEM((n * depth, width), bf16),
            pltpu.VMEM((length * rows, width), bf16),
            pltpu.VMEM((2 * rows, width), bf16),
            pltpu.VMEM((n, rows, depth), bf16),
            pltpu.VMEM((n, depth, rows), bf16),
            pltpu.VMEM((rows, feat), bf16),
            pltpu.VMEM((rows, width), bf16),
            pltpu.VMEM((2 * rows, length * rows), bf16),
            pltpu.VMEM((2, 1, 2 * rows), f32),
            pltpu.VMEM((length, 1, length * rows), f32),
            pltpu.VMEM((rows, width), bf16),
            pltpu.VMEM((rows, width), bf16),
            pltpu.VMEM((length, rows, width), f32),
            pltpu.VMEM((2, length - 1, rows, width), bf16),
            pltpu.VMEM((2, length - 1, rows, width), bf16),
            pltpu.VMEM((2, n - 1, depth, half), bf16),
            pltpu.VMEM((2, n - 1, depth, half), bf16),
            pltpu.SemaphoreType.DMA((3,)),
            pltpu.SemaphoreType.DMA((3,)),
            pltpu.SemaphoreType.DMA((2, 2, n - 1)),
            pltpu.SemaphoreType.DMA((2, 2, n - 1)),
            pltpu.SemaphoreType.DMA((3,)),
            pltpu.SemaphoreType.DMA((3,)),
            pltpu.SemaphoreType.DMA((length - 1,)),
            pltpu.SemaphoreType.DMA((length - 1,)),
            pltpu.SemaphoreType.DMA((2, 2, length - 1)),
            pltpu.SemaphoreType.DMA((2, 2, length - 1)),
        ],
        compiler_params=pltpu.CompilerParams(
            collective_id=0, has_side_effects=True, vmem_limit_bytes=62 * 2**20
        ),
    )(image_features, text_embed, image_head, logit_scale)
    return pl.pallas_call(
        hand_on_kernel,
        out_shape=out_shape,
        in_specs=[hbm, hbm, hbm],
        out_specs=(hbm, hbm, hbm),
        scratch_shapes=[
            pltpu.VMEM((rows, feat), bf16),
            pltpu.VMEM((rows, width), bf16),
            pltpu.VMEM((depth, width), f32),
            pltpu.SemaphoreType.DMA((2, 3)),
        ],
        compiler_params=pltpu.CompilerParams(vmem_limit_bytes=62 * 2**20),
    )(*results)


def fits_kernel(n, rows, width, depth, feat):
    pairs = n * rows
    size = 24 * pairs * rows + 4 * pairs * width + 8 * n * depth * width + 12 * rows * feat
    return (
        n % 2 == 0
        and n >= 6
        and rows % 128 == 0
        and width % 256 == 0
        and depth % 16 == 0
        and feat == n * depth
        and size <= 24 * 2**20
    )


def solution(mesh):
    n = mesh.shape["dp"]
    groups = mesh.shape["rep"] * n

    def step(image_features, text_embed, image_head, logit_scale):
        rows, width = text_embed.shape[0] // groups, text_embed.shape[1]
        depth, feat = image_head.shape[0] // groups, image_features.shape[1]
        if fits_kernel(n, rows, width, depth, feat):
            body = functools.partial(local_kernel, n)
        else:
            body = local
        split = P(("rep", "dp"), None)
        return jax.shard_map(
            body,
            mesh=mesh,
            in_specs=(split, split, split, P()),
            out_specs=(split, split, split),
            check_vma=False,
        )(image_features, text_embed, image_head, logit_scale)

    return step
```

```python
import functools

import jax
import jax.numpy as jnp
from jax import lax
from jax.experimental import pallas as pl
from jax.experimental.pallas import tpu as pltpu
from jax.sharding import PartitionSpec as P


def unit_rows(embedding):
    inv_norm = lax.rsqrt(jnp.sum(embedding * embedding, axis=1, keepdims=True) + 1e-06)
    return (embedding * inv_norm, inv_norm)


def norm_backward(embedding, inv_norm, upstream):
    inner = jnp.sum(embedding * upstream, axis=1, keepdims=True)
    return (inv_norm * upstream - embedding * (inv_norm * inv_norm * inv_norm) * inner).astype(
        jnp.bfloat16
    )


def tile_logits(logit_mult, left_rows, right_rows):
    product = lax.dot_general(
        left_rows, right_rows, (((1,), (1,)), ((), ())), preferred_element_type=jnp.float32
    )
    return logit_mult * product


def pair_coef(logits, left_lse, right_lse, left_ids, right_ids):
    label = (left_ids[:, None] == right_ids[None, :]).astype(jnp.float32)
    values = (
        jnp.exp(logits - left_lse[:, None]) + jnp.exp(logits - right_lse[None, :]) - 2.0 * label
    )
    return values.astype(jnp.bfloat16)


def local(image_features, text_embed, image_head, logit_scale):
    logit_mult = logit_scale[0]
    row_count = image_features.shape[0]
    own_ids = lax.axis_index("dp") * row_count + jnp.arange(row_count, dtype=jnp.int32)
    head_full = lax.all_gather(image_head, "dp", axis=0, tiled=True)
    img_emb = jnp.dot(image_features, head_full, preferred_element_type=jnp.float32)
    img_scaled, img_inv = unit_rows(img_emb)
    img_unit = img_scaled.astype(jnp.bfloat16)
    txt_emb = text_embed.astype(jnp.float32)
    txt_scaled, txt_inv = unit_rows(txt_emb)
    txt_unit = txt_scaled.astype(jnp.bfloat16)
    exp_tile = jnp.exp(
        tile_logits(logit_mult, img_unit, lax.all_gather(txt_unit, "dp", axis=0, tiled=True))
    )
    col_part = jnp.sum(exp_tile, axis=0)
    row_sum, col_part = (jnp.sum(exp_tile, axis=1), col_part)
    row_lse = jnp.log(row_sum)
    col_lse = jnp.log(lax.psum_scatter(col_part, "dp", scatter_dimension=0, tiled=True))
    row_all, col_all = (
        lax.all_gather(row_lse, "dp", axis=0, tiled=True),
        lax.all_gather(col_lse, "dp", axis=0, tiled=True),
    )
    img_piece = lax.all_gather(img_unit, "dp", axis=0, tiled=True)
    txt_piece = lax.all_gather(txt_unit, "dp", axis=0, tiled=True)
    count = img_piece.shape[0]
    piece_ids = jnp.arange(count, dtype=jnp.int32)
    img_coef = pair_coef(
        tile_logits(logit_mult, img_unit, txt_piece), row_lse, col_all, own_ids, piece_ids
    )
    txt_coef = pair_coef(
        tile_logits(logit_mult, txt_unit, img_piece), col_lse, row_all, own_ids, piece_ids
    )
    img_acc = jnp.dot(img_coef, txt_piece, preferred_element_type=jnp.float32)
    txt_acc = jnp.dot(txt_coef, img_piece, preferred_element_type=jnp.float32)
    img_unit_grad = logit_mult * img_acc
    txt_unit_grad = logit_mult * txt_acc
    img_emb_grad = norm_backward(img_emb, img_inv, img_unit_grad)
    text_embed_grad = norm_backward(txt_emb, txt_inv, txt_unit_grad)
    image_features_grad = lax.dot_general(
        img_emb_grad, head_full, (((1,), (1,)), ((), ())), preferred_element_type=jnp.float32
    ).astype(jnp.bfloat16)
    head_partial = lax.dot_general(
        image_features, img_emb_grad, (((0,), (0,)), ((), ())), preferred_element_type=jnp.float32
    )
    image_head_grad = lax.psum_scatter(
        head_partial.astype(jnp.bfloat16), "dp", scatter_dimension=0, tiled=True
    ).astype(jnp.float32)
    return (image_features_grad, text_embed_grad, image_head_grad)


MESH = pl.DeviceIdType.MESH
HEAD, GRAD = range(2)
IMAGES, IMAGE_GRADS, ROW_SUMS = range(3)
ROWS_ROWS = (((1,), (1,)), ((), ()))
COLS_COLS = (((0,), (0,)), ((), ()))


def place_of(index, n):
    depth, side = lax.div(index, 2), lax.rem(index, 2)
    return depth + side * (n - 1 - 2 * depth)


def index_at(place, n):
    place = lax.rem(place + 2 * n, n)
    side = lax.div(place, n // 2)
    return 2 * (place + side * (n - 1 - 2 * place)) + side


def step_kernel(
    n,
    feat_hbm,
    text_hbm,
    head_hbm,
    scale_ref,
    feat_out,
    text_out,
    head_out,
    feat_grad_ref,
    text_grad_ref,
    head_grad_ref,
    head_all,
    text_col,
    images,
    feat_blocks,
    feat_t_blocks,
    feat_ref,
    text_ref,
    coefs,
    row_stats,
    col_stats,
    image_out,
    image_in,
    text_part,
    text_going,
    text_coming,
    outgoing,
    incoming,
    load_sem,
    store_sem,
    send_sem,
    recv_sem,
    pair_send_sem,
    pair_recv_sem,
    stats_send_sem,
    stats_recv_sem,
    chain_send_sem,
    chain_recv_sem,
):
    rows, width = text_hbm.shape
    depth = head_hbm.shape[0]
    half = width // 2
    length = n // 2
    messages = n - 1
    me = lax.axis_index("dp")
    place = place_of(me, n)
    level, side = lax.div(me, 2), lax.rem(me, 2)
    other = me + 1 - 2 * side
    partner = {+1: index_at(place + 1, n), -1: index_at(place - 1, n)}

    own_head = pl.ds(pl.multiple_of(me * depth, 16), depth)
    loads = [
        pltpu.make_async_copy(
            head_hbm.at[:, pl.ds(c * half, half)], head_all.at[c, own_head, :], load_sem.at[2 + c]
        )
        for c in range(2)
    ] + [
        pltpu.make_async_copy(text_hbm, text_ref, load_sem.at[0]),
        pltpu.make_async_copy(feat_hbm, feat_ref, load_sem.at[1]),
    ]
    stores = [
        pltpu.make_async_copy(feat_grad_ref, feat_out, store_sem.at[0]),
        pltpu.make_async_copy(text_grad_ref, text_out, store_sem.at[1]),
        pltpu.make_async_copy(head_grad_ref, head_out, store_sem.at[2]),
    ]
    for load in loads:
        load.start()
    barrier = pltpu.get_barrier_semaphore()
    for k in range(1, n):
        pl.semaphore_signal(
            barrier, inc=1, device_id={"dp": lax.rem(me + k, n)}, device_id_type=MESH
        )
    loads[0].wait()
    loads[1].wait()
    pl.semaphore_wait(barrier, n - 1)

    def columns(way, m):
        first = (m % 2 == 0) == (way == 1)
        return pl.ds(0 if first else half, half)

    def remote(kind, way, m, src, dst):
        side = 0 if way == 1 else 1
        return pltpu.make_async_remote_copy(
            src_ref=src,
            dst_ref=dst,
            send_sem=send_sem.at[kind, side, m],
            recv_sem=recv_sem.at[kind, side, m],
            device_id={"dp": partner[way]},
            device_id_type=MESH,
        )

    gathered = {HEAD: (head_all, depth)}

    def gather_copy(kind, way, m, origin_shift):
        buf, block = gathered[kind]
        owner = index_at(place - way * origin_shift, n)
        at = pl.ds(pl.multiple_of(owner * block, 16), block)
        ref = buf.at[columns(way, m).start // half, at, :]
        return remote(kind, way, m, ref, ref)

    def gather_send(kind, m):
        for way in (1, -1):
            if m >= 2:
                gather_copy(kind, way, m - 2, m // 2).wait_recv()
            gather_copy(kind, way, m, m // 2).start()

    def gather_last(kind):
        for m in range(max(messages - 2, 0), messages):
            for way in (1, -1):
                gather_copy(kind, way, m, m // 2 + 1).wait_recv()

    def along(way):
        return level if way == 1 else length - 1 - level

    def chain_copy(kind, way, slot, src, dst):
        return pltpu.make_async_remote_copy(
            src_ref=src,
            dst_ref=dst,
            send_sem=chain_send_sem.at[kind, 0 if way == 1 else 1, slot],
            recv_sem=chain_recv_sem.at[kind, 0 if way == 1 else 1, slot],
            device_id={"dp": lax.rem(me + 2 * way + n, n)},
            device_id_type=MESH,
        )

    def text_copy(way, slot, shift):
        owner = level - way * shift
        ref = text_col.at[pl.ds(pl.multiple_of(owner * rows, 16), rows), :]
        return chain_copy(0, way, slot, ref, ref)

    def text_slot(slot):
        for way in (1, -1):
            if slot >= 1:

                @pl.when(along(way) >= slot)
                def _():
                    text_copy(way, slot - 1, slot).wait_recv()

            if slot <= length - 2:

                @pl.when((along(way) >= slot) & (along(way) < length - 1))
                def _():
                    text_copy(way, slot, slot).start()

    def pair_copy(kind, src, dst):
        return pltpu.make_async_remote_copy(
            src_ref=src,
            dst_ref=dst,
            send_sem=pair_send_sem.at[kind],
            recv_sem=pair_recv_sem.at[kind],
            device_id={"dp": other},
            device_id_type=MESH,
        )

    own_images = pl.ds(pl.multiple_of(side * rows, 16), rows)
    other_images = pl.ds(pl.multiple_of((1 - side) * rows, 16), rows)
    images_copy = pair_copy(IMAGES, images.at[own_images, :], images.at[own_images, :])
    images_landed = pair_copy(IMAGES, images.at[other_images, :], images.at[other_images, :])
    grads_copy = pair_copy(IMAGE_GRADS, image_out, image_in)
    sums_copy = pair_copy(ROW_SUMS, row_stats.at[side], row_stats.at[side])
    sums_landed = pair_copy(ROW_SUMS, row_stats.at[1 - side], row_stats.at[1 - side])

    gather_send(HEAD, 0)
    gather_send(HEAD, 1)

    loads[2].wait()
    txt_emb = text_ref[...].astype(jnp.float32)
    txt_scaled, txt_inv = unit_rows(txt_emb)
    text_col[pl.ds(pl.multiple_of(level * rows, 16), rows), :] = txt_scaled.astype(jnp.bfloat16)
    gather_send(HEAD, 2)
    loads[3].wait()
    feat_t = feat_ref[...].astype(jnp.float32).T

    def split_feat(first, last):
        for b in range(first, last):
            block = feat_t[b * depth : (b + 1) * depth]
            feat_t_blocks[b] = block.astype(jnp.bfloat16)
            feat_blocks[b] = block.T.astype(jnp.bfloat16)

    split_feat(0, n // 2)
    gather_send(HEAD, 3)
    split_feat(n // 2, n)

    def emb_part(owner):
        at = pl.ds(pl.multiple_of(owner * depth, 16), depth)
        block = feat_blocks[owner]
        return jnp.concatenate(
            [
                jnp.dot(block, head_all[c, at, :], preferred_element_type=jnp.float32)
                for c in range(2)
            ],
            axis=1,
        )

    def emb_parts(shift):
        return emb_part(index_at(place - shift, n)) + emb_part(index_at(place + shift, n))

    gather_send(HEAD, 4)
    img_emb = emb_part(me) + emb_parts(1)
    for m in range(5, messages):
        gather_send(HEAD, m)
        if m % 2 == 1:
            img_emb += emb_parts(m // 2)
        if m == messages - 2:
            text_slot(0)
    gather_last(HEAD)
    text_slot(1)
    img_emb += emb_parts(n // 2 - 1)
    img_emb += emb_part(index_at(place + n // 2, n))
    img_scaled, img_inv = unit_rows(img_emb)
    img_unit = img_scaled.astype(jnp.bfloat16)
    images[own_images, :] = img_unit
    images_copy.start()
    for slot in range(2, length):
        text_slot(slot)

    scale = scale_ref[0]
    own_exp = jnp.exp(tile_logits(scale, img_unit, text_col[...]))
    images_landed.wait_recv()
    other_exp = jnp.exp(tile_logits(scale, images[other_images, :], text_col[...]))
    exp_tile = jnp.concatenate(
        [jnp.where(side == 0, own_exp, other_exp), jnp.where(side == 0, other_exp, own_exp)], axis=0
    )
    row_part = jnp.sum(exp_tile, axis=1, keepdims=True)
    row_stats[side] = jnp.broadcast_to(row_part, (2 * rows, rows)).T[0:1, :]
    col_stats[level] = jnp.sum(exp_tile, axis=0, keepdims=True)

    def stats_copy(k, sender):
        return pltpu.make_async_remote_copy(
            src_ref=col_stats.at[sender],
            dst_ref=col_stats.at[sender],
            send_sem=stats_send_sem.at[k - 1],
            recv_sem=stats_recv_sem.at[k - 1],
            device_id={"dp": 2 * lax.rem(level + k, length) + side},
            device_id_type=MESH,
        )

    for k in range(1, length):
        stats_copy(k, level).start()
    sums_copy.start()
    sums_landed.wait_recv()
    inv_row = 1.0 / jnp.broadcast_to(row_stats[0] + row_stats[1], (rows, 2 * rows)).T[:, 0:1]
    tile = (2 * rows, length * rows)
    row_ids = lax.broadcasted_iota(jnp.int32, tile, 0) - side * rows
    col_ids = lax.broadcasted_iota(jnp.int32, tile, 1) - level * rows
    label = (row_ids == col_ids) & (row_ids >= 0) & (row_ids < rows)
    minus = jnp.where(label, 2.0, 0.0)
    for k in range(1, length):
        stats_copy(k, lax.rem(level - k + length, length)).wait_recv()
    col_sum = col_stats[0]
    for k in range(1, length):
        col_sum += col_stats[k]
    coefs[...] = (exp_tile * (inv_row + 1.0 / col_sum) - minus).astype(jnp.bfloat16)

    image_out[...] = jnp.dot(
        coefs[other_images, :], text_col[...], preferred_element_type=jnp.float32
    ).astype(jnp.bfloat16)
    grads_copy.start()
    text_acc = lax.dot_general(
        coefs[...], images[...], COLS_COLS, preferred_element_type=jnp.float32
    )
    for b in range(length):
        text_part[b] = text_acc[b * rows : (b + 1) * rows]

    def text_grad_copy(way, slot):
        which = 0 if way == 1 else 1
        return chain_copy(1, way, slot, text_going.at[which, slot], text_coming.at[which, slot])

    def text_grad_slot(slot):
        for way in (1, -1):
            which = 0 if way == 1 else 1

            @pl.when(along(way) <= slot)
            def _():
                ahead = length - 1 - slot + along(way)
                value = text_part[ahead if way == 1 else length - 1 - ahead]
                text_going[which, slot] = value.astype(jnp.bfloat16)

            if slot >= 1:

                @pl.when((along(way) <= slot) & (along(way) >= 1))
                def _():
                    ahead = length - 1 - slot + along(way)
                    value = text_part[ahead if way == 1 else length - 1 - ahead]
                    text_grad_copy(way, slot - 1).wait_recv()
                    value += text_coming[which, slot - 1].astype(jnp.float32)
                    text_going[which, slot] = value.astype(jnp.bfloat16)

            @pl.when(along(way) <= slot)
            def _():
                text_grad_copy(way, slot).start()

    text_grad_slot(0)
    img_acc = jnp.dot(
        coefs[own_images, :], text_col[...], preferred_element_type=jnp.float32
    )
    grads_copy.wait_recv()
    img_acc += image_in[...].astype(jnp.float32)
    img_emb_grad = norm_backward(img_emb, img_inv, scale * img_acc)

    def head_part(owner, cols):
        return jnp.dot(
            feat_t_blocks[owner],
            img_emb_grad[:, cols.start : cols.start + half],
            preferred_element_type=jnp.float32,
        )

    def grad_copy(way, m):
        side = 0 if way == 1 else 1
        return remote(GRAD, way, m, outgoing.at[side, m], incoming.at[side, m])

    def grad_send(m):
        for way in (1, -1):
            side = 0 if way == 1 else 1
            value = head_part(index_at(place + way * (n // 2 - (m + 1) // 2), n), columns(way, m))
            if m >= 2:
                grad_copy(way, m - 2).wait_recv()
                value += incoming[side, m - 2].astype(jnp.float32)
            outgoing[side, m] = value.astype(jnp.bfloat16)
            grad_copy(way, m).start()

    def text_side():
        for way in (1, -1):
            which = 0 if way == 1 else 1

            @pl.when(along(way) >= 1)
            def _():
                text_grad_copy(way, length - 2).wait_recv()
                text_part[level] += text_coming[which, length - 2].astype(jnp.float32)

        text_grad_ref[...] = norm_backward(txt_emb, txt_inv, scale * text_part[level])
        stores[1].start()

    def feat_side():
        feat_grad_ref[...] = sum(
            lax.dot_general(
                img_emb_grad[:, c * half : (c + 1) * half],
                head_all[c],
                ROWS_ROWS,
                preferred_element_type=jnp.float32,
            )
            for c in range(2)
        ).astype(jnp.bfloat16)
        stores[0].start()

    for m in range(messages):
        grad_send(m)
        if m >= 1 and m <= length - 2:
            text_grad_slot(m)
    feat_side()
    text_side()

    total = [head_part(me, pl.ds(0, half)), head_part(me, pl.ds(half, half))]
    for m in range(messages - 2, messages):
        for way in (1, -1):
            grad_copy(way, m).wait_recv()
            which = columns(way, m).start // half
            total[which] += incoming[0 if way == 1 else 1, m].astype(jnp.float32)
    head_grad_ref[:, 0:half] = total[0]
    head_grad_ref[:, half:width] = total[1]
    stores[2].start()

    for m in range(messages):
        for way in (1, -1):
            for kind in gathered:
                gather_copy(kind, way, m, m // 2).wait_send()
            grad_copy(way, m).wait_send()
    for k in range(1, length):
        stats_copy(k, level).wait_send()
    images_copy.wait_send()
    grads_copy.wait_send()
    sums_copy.wait_send()
    for way in (1, -1):
        for slot in range(length - 1):

            @pl.when((along(way) >= slot) & (along(way) < length - 1))
            def _():
                text_copy(way, slot, slot).wait_send()

            @pl.when(along(way) <= slot)
            def _():
                text_grad_copy(way, slot).wait_send()

    for store in stores:
        store.wait()


def hand_on_kernel(*refs):
    sources, results, held, sem = refs[:3], refs[3:6], refs[6:9], refs[9]
    loads = [pltpu.make_async_copy(sources[i], held[i], sem.at[0, i]) for i in range(3)]
    stores = [pltpu.make_async_copy(held[i], results[i], sem.at[1, i]) for i in range(3)]
    for load in loads:
        load.start()
    for load, store in zip(loads, stores):
        load.wait()
        store.start()
    for store in stores:
        store.wait()


def local_kernel(n, image_features, text_embed, image_head, logit_scale):
    rows, width = text_embed.shape
    depth, feat = image_head.shape[0], image_features.shape[1]
    length = n // 2
    half = width // 2
    bf16, f32 = jnp.bfloat16, jnp.float32
    hbm = pl.BlockSpec(memory_space=pltpu.HBM)
    out_shape = (
        jax.ShapeDtypeStruct((rows, feat), bf16),
        jax.ShapeDtypeStruct((rows, width), bf16),
        jax.ShapeDtypeStruct((depth, width), f32),
    )
    results = pl.pallas_call(
        functools.partial(step_kernel, n),
        out_shape=out_shape,
        in_specs=[hbm, hbm, hbm, pl.BlockSpec(memory_space=pltpu.SMEM)],
        out_specs=(hbm, hbm, hbm),
        scratch_shapes=[
            pltpu.VMEM((rows, feat), bf16),
            pltpu.VMEM((rows, width), bf16),
            pltpu.VMEM((depth, width), f32),
            pltpu.VMEM((2, n * depth, half), bf16),
            pltpu.VMEM((length * rows, width), bf16),
            pltpu.VMEM((2 * rows, width), bf16),
            pltpu.VMEM((n, rows, depth), bf16),
            pltpu.VMEM((n, depth, rows), bf16),
            pltpu.VMEM((rows, feat), bf16),
            pltpu.VMEM((rows, width), bf16),
            pltpu.VMEM((2 * rows, length * rows), bf16),
            pltpu.VMEM((2, 1, 2 * rows), f32),
            pltpu.VMEM((length, 1, length * rows), f32),
            pltpu.VMEM((rows, width), bf16),
            pltpu.VMEM((rows, width), bf16),
            pltpu.VMEM((length, rows, width), f32),
            pltpu.VMEM((2, length - 1, rows, width), bf16),
            pltpu.VMEM((2, length - 1, rows, width), bf16),
            pltpu.VMEM((2, n - 1, depth, half), bf16),
            pltpu.VMEM((2, n - 1, depth, half), bf16),
            pltpu.SemaphoreType.DMA((4,)),
            pltpu.SemaphoreType.DMA((3,)),
            pltpu.SemaphoreType.DMA((2, 2, n - 1)),
            pltpu.SemaphoreType.DMA((2, 2, n - 1)),
            pltpu.SemaphoreType.DMA((3,)),
            pltpu.SemaphoreType.DMA((3,)),
            pltpu.SemaphoreType.DMA((length - 1,)),
            pltpu.SemaphoreType.DMA((length - 1,)),
            pltpu.SemaphoreType.DMA((2, 2, length - 1)),
            pltpu.SemaphoreType.DMA((2, 2, length - 1)),
        ],
        compiler_params=pltpu.CompilerParams(
            collective_id=0, has_side_effects=True, vmem_limit_bytes=62 * 2**20
        ),
    )(image_features, text_embed, image_head, logit_scale)
    return pl.pallas_call(
        hand_on_kernel,
        out_shape=out_shape,
        in_specs=[hbm, hbm, hbm],
        out_specs=(hbm, hbm, hbm),
        scratch_shapes=[
            pltpu.VMEM((rows, feat), bf16),
            pltpu.VMEM((rows, width), bf16),
            pltpu.VMEM((depth, width), f32),
            pltpu.SemaphoreType.DMA((2, 3)),
        ],
        compiler_params=pltpu.CompilerParams(vmem_limit_bytes=62 * 2**20),
    )(*results)


def fits_kernel(n, rows, width, depth, feat):
    pairs = n * rows
    size = 24 * pairs * rows + 4 * pairs * width + 8 * n * depth * width + 12 * rows * feat
    return (
        n % 2 == 0
        and n >= 8
        and rows % 128 == 0
        and width % 256 == 0
        and depth % 16 == 0
        and feat == n * depth
        and size <= 24 * 2**20
    )


def solution(mesh):
    n = mesh.shape["dp"]
    groups = mesh.shape["rep"] * n

    def step(image_features, text_embed, image_head, logit_scale):
        rows, width = text_embed.shape[0] // groups, text_embed.shape[1]
        depth, feat = image_head.shape[0] // groups, image_features.shape[1]
        if fits_kernel(n, rows, width, depth, feat):
            body = functools.partial(local_kernel, n)
        else:
            body = local
        split = P(("rep", "dp"), None)
        return jax.shard_map(
            body,
            mesh=mesh,
            in_specs=(split, split, split, P()),
            out_specs=(split, split, split),
            check_vma=False,
        )(image_features, text_embed, image_head, logit_scale)

    return step
```

```python
import functools

import jax
import jax.numpy as jnp
from jax import lax
from jax.experimental import pallas as pl
from jax.experimental.pallas import tpu as pltpu
from jax.sharding import PartitionSpec as P


def unit_rows(embedding):
    inv_norm = lax.rsqrt(jnp.sum(embedding * embedding, axis=1, keepdims=True) + 1e-06)
    return (embedding * inv_norm, inv_norm)


def norm_backward(embedding, inv_norm, upstream):
    inner = jnp.sum(embedding * upstream, axis=1, keepdims=True)
    return (inv_norm * upstream - embedding * (inv_norm * inv_norm * inv_norm) * inner).astype(
        jnp.bfloat16
    )


def tile_logits(logit_mult, left_rows, right_rows):
    product = lax.dot_general(
        left_rows, right_rows, (((1,), (1,)), ((), ())), preferred_element_type=jnp.float32
    )
    return logit_mult * product


def pair_coef(logits, left_lse, right_lse, left_ids, right_ids):
    label = (left_ids[:, None] == right_ids[None, :]).astype(jnp.float32)
    values = (
        jnp.exp(logits - left_lse[:, None]) + jnp.exp(logits - right_lse[None, :]) - 2.0 * label
    )
    return values.astype(jnp.bfloat16)


def local(image_features, text_embed, image_head, logit_scale):
    logit_mult = logit_scale[0]
    row_count = image_features.shape[0]
    own_ids = lax.axis_index("dp") * row_count + jnp.arange(row_count, dtype=jnp.int32)
    head_full = lax.all_gather(image_head, "dp", axis=0, tiled=True)
    img_emb = jnp.dot(image_features, head_full, preferred_element_type=jnp.float32)
    img_scaled, img_inv = unit_rows(img_emb)
    img_unit = img_scaled.astype(jnp.bfloat16)
    txt_emb = text_embed.astype(jnp.float32)
    txt_scaled, txt_inv = unit_rows(txt_emb)
    txt_unit = txt_scaled.astype(jnp.bfloat16)
    exp_tile = jnp.exp(
        tile_logits(logit_mult, img_unit, lax.all_gather(txt_unit, "dp", axis=0, tiled=True))
    )
    col_part = jnp.sum(exp_tile, axis=0)
    row_sum, col_part = (jnp.sum(exp_tile, axis=1), col_part)
    row_lse = jnp.log(row_sum)
    col_lse = jnp.log(lax.psum_scatter(col_part, "dp", scatter_dimension=0, tiled=True))
    row_all, col_all = (
        lax.all_gather(row_lse, "dp", axis=0, tiled=True),
        lax.all_gather(col_lse, "dp", axis=0, tiled=True),
    )
    img_piece = lax.all_gather(img_unit, "dp", axis=0, tiled=True)
    txt_piece = lax.all_gather(txt_unit, "dp", axis=0, tiled=True)
    count = img_piece.shape[0]
    piece_ids = jnp.arange(count, dtype=jnp.int32)
    img_coef = pair_coef(
        tile_logits(logit_mult, img_unit, txt_piece), row_lse, col_all, own_ids, piece_ids
    )
    txt_coef = pair_coef(
        tile_logits(logit_mult, txt_unit, img_piece), col_lse, row_all, own_ids, piece_ids
    )
    img_acc = jnp.dot(img_coef, txt_piece, preferred_element_type=jnp.float32)
    txt_acc = jnp.dot(txt_coef, img_piece, preferred_element_type=jnp.float32)
    img_unit_grad = logit_mult * img_acc
    txt_unit_grad = logit_mult * txt_acc
    img_emb_grad = norm_backward(img_emb, img_inv, img_unit_grad)
    text_embed_grad = norm_backward(txt_emb, txt_inv, txt_unit_grad)
    image_features_grad = lax.dot_general(
        img_emb_grad, head_full, (((1,), (1,)), ((), ())), preferred_element_type=jnp.float32
    ).astype(jnp.bfloat16)
    head_partial = lax.dot_general(
        image_features, img_emb_grad, (((0,), (0,)), ((), ())), preferred_element_type=jnp.float32
    )
    image_head_grad = lax.psum_scatter(
        head_partial.astype(jnp.bfloat16), "dp", scatter_dimension=0, tiled=True
    ).astype(jnp.float32)
    return (image_features_grad, text_embed_grad, image_head_grad)


MESH = pl.DeviceIdType.MESH
CHUNKS = 4
HEAD, GRAD = range(2)
IMAGES, IMAGE_GRADS, ROW_SUMS = range(3)
ROWS_ROWS = (((1,), (1,)), ((), ()))
COLS_COLS = (((0,), (0,)), ((), ()))


def place_of(index, n):
    depth, side = lax.div(index, 2), lax.rem(index, 2)
    return depth + side * (n - 1 - 2 * depth)


def index_at(place, n):
    place = lax.rem(place + 2 * n, n)
    side = lax.div(place, n // 2)
    return 2 * (place + side * (n - 1 - 2 * place)) + side


def step_kernel(
    n,
    feat_hbm,
    text_hbm,
    head_hbm,
    scale_ref,
    feat_out,
    text_out,
    head_out,
    feat_grad_ref,
    text_grad_ref,
    head_grad_ref,
    head_all,
    text_col,
    images,
    feat_blocks,
    feat_t_blocks,
    feat_ref,
    text_ref,
    coefs,
    row_stats,
    col_stats,
    image_out,
    image_in,
    text_part,
    text_going,
    text_coming,
    outgoing,
    incoming,
    load_sem,
    store_sem,
    send_sem,
    recv_sem,
    pair_send_sem,
    pair_recv_sem,
    stats_send_sem,
    stats_recv_sem,
    chain_send_sem,
    chain_recv_sem,
):
    rows, width = text_hbm.shape
    depth = head_hbm.shape[0]
    chunk = width // CHUNKS
    length = n // 2
    messages = CHUNKS * (n - 1) // 2
    me = lax.axis_index("dp")
    place = place_of(me, n)
    level, side = lax.div(me, 2), lax.rem(me, 2)
    other = me + 1 - 2 * side
    partner = {+1: index_at(place + 1, n), -1: index_at(place - 1, n)}

    own_head = pl.ds(pl.multiple_of(me * depth, 16), depth)
    loads = [
        pltpu.make_async_copy(head_hbm, head_all.at[own_head, :], load_sem.at[2]),
        pltpu.make_async_copy(text_hbm, text_ref, load_sem.at[0]),
        pltpu.make_async_copy(feat_hbm, feat_ref, load_sem.at[1]),
    ]
    stores = [
        pltpu.make_async_copy(feat_grad_ref, feat_out, store_sem.at[0]),
        pltpu.make_async_copy(text_grad_ref, text_out, store_sem.at[1]),
        pltpu.make_async_copy(head_grad_ref, head_out, store_sem.at[2]),
    ]
    for load in loads:
        load.start()
    barrier = pltpu.get_barrier_semaphore()
    for k in range(1, n):
        pl.semaphore_signal(
            barrier, inc=1, device_id={"dp": lax.rem(me + k, n)}, device_id_type=MESH
        )
    loads[0].wait()
    pl.semaphore_wait(barrier, n - 1)

    def columns(way, m):
        return pl.ds((m % CHUNKS + (0 if way == 1 else CHUNKS // 2)) % CHUNKS * chunk, chunk)

    def remote(kind, way, m, src, dst):
        side = 0 if way == 1 else 1
        return pltpu.make_async_remote_copy(
            src_ref=src,
            dst_ref=dst,
            send_sem=send_sem.at[kind, side, m],
            recv_sem=recv_sem.at[kind, side, m],
            device_id={"dp": partner[way]},
            device_id_type=MESH,
        )

    gathered = {HEAD: (head_all, depth)}

    def gather_copy(kind, way, m, origin_shift):
        buf, block = gathered[kind]
        owner = index_at(place - way * origin_shift, n)
        at = pl.ds(pl.multiple_of(owner * block, 16), block)
        ref = buf.at[at, columns(way, m)]
        return remote(kind, way, m, ref, ref)

    def gather_send(kind, step):
        for m in range(step * CHUNKS, min((step + 1) * CHUNKS, messages)):
            for way in (1, -1):
                if step >= 1:
                    gather_copy(kind, way, m - CHUNKS, step).wait_recv()
                gather_copy(kind, way, m, step).start()

    def gather_last(kind):
        for m in range(messages - CHUNKS, messages):
            for way in (1, -1):
                gather_copy(kind, way, m, m // CHUNKS + 1).wait_recv()

    def along(way):
        return level if way == 1 else length - 1 - level

    def chain_copy(kind, way, slot, src, dst):
        return pltpu.make_async_remote_copy(
            src_ref=src,
            dst_ref=dst,
            send_sem=chain_send_sem.at[kind, 0 if way == 1 else 1, slot],
            recv_sem=chain_recv_sem.at[kind, 0 if way == 1 else 1, slot],
            device_id={"dp": lax.rem(me + 2 * way + n, n)},
            device_id_type=MESH,
        )

    def text_copy(way, slot, shift):
        owner = level - way * shift
        ref = text_col.at[pl.ds(pl.multiple_of(owner * rows, 16), rows), :]
        return chain_copy(0, way, slot, ref, ref)

    def text_slot(slot):
        for way in (1, -1):
            if slot >= 1:

                @pl.when(along(way) >= slot)
                def _():
                    text_copy(way, slot - 1, slot).wait_recv()

            if slot <= length - 2:

                @pl.when((along(way) >= slot) & (along(way) < length - 1))
                def _():
                    text_copy(way, slot, slot).start()

    def pair_copy(kind, src, dst):
        return pltpu.make_async_remote_copy(
            src_ref=src,
            dst_ref=dst,
            send_sem=pair_send_sem.at[kind],
            recv_sem=pair_recv_sem.at[kind],
            device_id={"dp": other},
            device_id_type=MESH,
        )

    own_images = pl.ds(pl.multiple_of(side * rows, 16), rows)
    other_images = pl.ds(pl.multiple_of((1 - side) * rows, 16), rows)
    images_copy = pair_copy(IMAGES, images.at[own_images, :], images.at[own_images, :])
    images_landed = pair_copy(IMAGES, images.at[other_images, :], images.at[other_images, :])
    grads_copy = pair_copy(IMAGE_GRADS, image_out, image_in)
    sums_copy = pair_copy(ROW_SUMS, row_stats.at[side], row_stats.at[side])
    sums_landed = pair_copy(ROW_SUMS, row_stats.at[1 - side], row_stats.at[1 - side])

    gather_send(HEAD, 0)

    loads[1].wait()
    txt_emb = text_ref[...].astype(jnp.float32)
    txt_scaled, txt_inv = unit_rows(txt_emb)
    text_col[pl.ds(pl.multiple_of(level * rows, 16), rows), :] = txt_scaled.astype(jnp.bfloat16)
    text_slot(0)
    loads[2].wait()
    feat_t = feat_ref[...].astype(jnp.float32).T
    for b in range(n):
        block = feat_t[b * depth : (b + 1) * depth]
        feat_t_blocks[b] = block.astype(jnp.bfloat16)
        feat_blocks[b] = block.T.astype(jnp.bfloat16)

    def emb_part(owner):
        at = pl.ds(pl.multiple_of(owner * depth, 16), depth)
        block = feat_blocks[owner]
        return jnp.dot(block, head_all[at, :], preferred_element_type=jnp.float32)

    def emb_parts(shift):
        return emb_part(index_at(place - shift, n)) + emb_part(index_at(place + shift, n))

    img_emb = None
    for step in range(1, length):
        gather_send(HEAD, step)
        if step < length - 1:
            text_slot(step)
        part = emb_parts(step - 1) if step > 1 else emb_part(me)
        img_emb = part if img_emb is None else img_emb + part
    gather_last(HEAD)
    img_emb += emb_parts(length - 1)
    img_emb += emb_part(index_at(place + length, n))
    img_scaled, img_inv = unit_rows(img_emb)
    img_unit = img_scaled.astype(jnp.bfloat16)
    images[own_images, :] = img_unit
    images_copy.start()
    text_slot(length - 1)

    scale = scale_ref[0]
    own_exp = jnp.exp(tile_logits(scale, img_unit, text_col[...]))
    images_landed.wait_recv()
    other_exp = jnp.exp(tile_logits(scale, images[other_images, :], text_col[...]))
    exp_tile = jnp.concatenate(
        [jnp.where(side == 0, own_exp, other_exp), jnp.where(side == 0, other_exp, own_exp)], axis=0
    )
    row_part = jnp.sum(exp_tile, axis=1, keepdims=True)
    row_stats[side] = jnp.broadcast_to(row_part, (2 * rows, rows)).T[0:1, :]
    col_stats[level] = jnp.sum(exp_tile, axis=0, keepdims=True)

    def stats_copy(k, sender):
        return pltpu.make_async_remote_copy(
            src_ref=col_stats.at[sender],
            dst_ref=col_stats.at[sender],
            send_sem=stats_send_sem.at[k - 1],
            recv_sem=stats_recv_sem.at[k - 1],
            device_id={"dp": 2 * lax.rem(level + k, length) + side},
            device_id_type=MESH,
        )

    for k in range(1, length):
        stats_copy(k, level).start()
    sums_copy.start()
    sums_landed.wait_recv()
    inv_row = 1.0 / jnp.broadcast_to(row_stats[0] + row_stats[1], (rows, 2 * rows)).T[:, 0:1]
    tile = (2 * rows, length * rows)
    row_ids = lax.broadcasted_iota(jnp.int32, tile, 0) - side * rows
    col_ids = lax.broadcasted_iota(jnp.int32, tile, 1) - level * rows
    label = (row_ids == col_ids) & (row_ids >= 0) & (row_ids < rows)
    minus = jnp.where(label, 2.0, 0.0)
    for k in range(1, length):
        stats_copy(k, lax.rem(level - k + length, length)).wait_recv()
    col_sum = col_stats[0]
    for k in range(1, length):
        col_sum += col_stats[k]
    coefs[...] = (exp_tile * (inv_row + 1.0 / col_sum) - minus).astype(jnp.bfloat16)

    image_out[...] = jnp.dot(
        coefs[other_images, :], text_col[...], preferred_element_type=jnp.float32
    ).astype(jnp.bfloat16)
    grads_copy.start()
    text_acc = lax.dot_general(
        coefs[...], images[...], COLS_COLS, preferred_element_type=jnp.float32
    )
    for b in range(length):
        text_part[b] = text_acc[b * rows : (b + 1) * rows]

    def text_grad_copy(way, slot):
        which = 0 if way == 1 else 1
        return chain_copy(1, way, slot, text_going.at[which, slot], text_coming.at[which, slot])

    def text_grad_slot(slot):
        for way in (1, -1):
            which = 0 if way == 1 else 1

            @pl.when(along(way) <= slot)
            def _():
                ahead = length - 1 - slot + along(way)
                value = text_part[ahead if way == 1 else length - 1 - ahead]
                text_going[which, slot] = value.astype(jnp.bfloat16)

            if slot >= 1:

                @pl.when((along(way) <= slot) & (along(way) >= 1))
                def _():
                    ahead = length - 1 - slot + along(way)
                    value = text_part[ahead if way == 1 else length - 1 - ahead]
                    text_grad_copy(way, slot - 1).wait_recv()
                    value += text_coming[which, slot - 1].astype(jnp.float32)
                    text_going[which, slot] = value.astype(jnp.bfloat16)

            @pl.when(along(way) <= slot)
            def _():
                text_grad_copy(way, slot).start()

    text_grad_slot(0)
    img_acc = jnp.dot(
        coefs[own_images, :], text_col[...], preferred_element_type=jnp.float32
    )
    grads_copy.wait_recv()
    img_acc += image_in[...].astype(jnp.float32)
    img_emb_grad = norm_backward(img_emb, img_inv, scale * img_acc)

    def head_part(owner, cols):
        return jnp.dot(
            feat_t_blocks[owner],
            img_emb_grad[:, cols.start : cols.start + cols.size],
            preferred_element_type=jnp.float32,
        )

    def grad_copy(way, m):
        side = 0 if way == 1 else 1
        return remote(GRAD, way, m, outgoing.at[side, m], incoming.at[side, m])

    def grad_send(step):
        for m in range(step * CHUNKS, min((step + 1) * CHUNKS, messages)):
            far = length - step - (0 if m % CHUNKS < CHUNKS // 2 else 1)
            for way in (1, -1):
                side = 0 if way == 1 else 1
                value = head_part(index_at(place + way * far, n), columns(way, m))
                if step >= 1:
                    grad_copy(way, m - CHUNKS).wait_recv()
                    value += incoming[side, m - CHUNKS].astype(jnp.float32)
                outgoing[side, m] = value.astype(jnp.bfloat16)
                grad_copy(way, m).start()

    def text_side():
        for way in (1, -1):
            which = 0 if way == 1 else 1

            @pl.when(along(way) >= 1)
            def _():
                text_grad_copy(way, length - 2).wait_recv()
                text_part[level] += text_coming[which, length - 2].astype(jnp.float32)

        text_grad_ref[...] = norm_backward(txt_emb, txt_inv, scale * text_part[level])
        stores[1].start()

    def feat_side():
        feat_grad_ref[...] = lax.dot_general(
            img_emb_grad, head_all[...], ROWS_ROWS, preferred_element_type=jnp.float32
        ).astype(jnp.bfloat16)
        stores[0].start()

    for step in range(length):
        grad_send(step)
        if 1 <= step <= length - 2:
            text_grad_slot(step)
    feat_side()
    text_side()

    total = head_part(me, pl.ds(0, width))
    arrived = {0: [None] * CHUNKS, 1: [None] * CHUNKS}
    for m in range(messages - CHUNKS, messages):
        for way in (1, -1):
            grad_copy(way, m).wait_recv()
            which = 0 if way == 1 else 1
            arrived[which][columns(way, m).start // chunk] = incoming[which, m].astype(jnp.float32)
    head_grad_ref[...] = (
        total + jnp.concatenate(arrived[0], axis=1) + jnp.concatenate(arrived[1], axis=1)
    )
    stores[2].start()

    for m in range(messages):
        for way in (1, -1):
            for kind in gathered:
                gather_copy(kind, way, m, m // 2).wait_send()
            grad_copy(way, m).wait_send()
    for k in range(1, length):
        stats_copy(k, level).wait_send()
    images_copy.wait_send()
    grads_copy.wait_send()
    sums_copy.wait_send()
    for way in (1, -1):
        for slot in range(length - 1):

            @pl.when((along(way) >= slot) & (along(way) < length - 1))
            def _():
                text_copy(way, slot, slot).wait_send()

            @pl.when(along(way) <= slot)
            def _():
                text_grad_copy(way, slot).wait_send()

    for store in stores:
        store.wait()


def hand_on_kernel(*refs):
    sources, results, held, sem = refs[:3], refs[3:6], refs[6:9], refs[9]
    loads = [pltpu.make_async_copy(sources[i], held[i], sem.at[0, i]) for i in range(3)]
    stores = [pltpu.make_async_copy(held[i], results[i], sem.at[1, i]) for i in range(3)]
    for load in loads:
        load.start()
    for load, store in zip(loads, stores):
        load.wait()
        store.start()
    for store in stores:
        store.wait()


def local_kernel(n, image_features, text_embed, image_head, logit_scale):
    rows, width = text_embed.shape
    depth, feat = image_head.shape[0], image_features.shape[1]
    length = n // 2
    chunk = width // CHUNKS
    messages = CHUNKS * (n - 1) // 2
    bf16, f32 = jnp.bfloat16, jnp.float32
    hbm = pl.BlockSpec(memory_space=pltpu.HBM)
    out_shape = (
        jax.ShapeDtypeStruct((rows, feat), bf16),
        jax.ShapeDtypeStruct((rows, width), bf16),
        jax.ShapeDtypeStruct((depth, width), f32),
    )
    results = pl.pallas_call(
        functools.partial(step_kernel, n),
        out_shape=out_shape,
        in_specs=[hbm, hbm, hbm, pl.BlockSpec(memory_space=pltpu.SMEM)],
        out_specs=(hbm, hbm, hbm),
        scratch_shapes=[
            pltpu.VMEM((rows, feat), bf16),
            pltpu.VMEM((rows, width), bf16),
            pltpu.VMEM((depth, width), f32),
            pltpu.VMEM((n * depth, width), bf16),
            pltpu.VMEM((length * rows, width), bf16),
            pltpu.VMEM((2 * rows, width), bf16),
            pltpu.VMEM((n, rows, depth), bf16),
            pltpu.VMEM((n, depth, rows), bf16),
            pltpu.VMEM((rows, feat), bf16),
            pltpu.VMEM((rows, width), bf16),
            pltpu.VMEM((2 * rows, length * rows), bf16),
            pltpu.VMEM((2, 1, 2 * rows), f32),
            pltpu.VMEM((length, 1, length * rows), f32),
            pltpu.VMEM((rows, width), bf16),
            pltpu.VMEM((rows, width), bf16),
            pltpu.VMEM((length, rows, width), f32),
            pltpu.VMEM((2, length - 1, rows, width), bf16),
            pltpu.VMEM((2, length - 1, rows, width), bf16),
            pltpu.VMEM((2, messages, depth, chunk), bf16),
            pltpu.VMEM((2, messages, depth, chunk), bf16),
            pltpu.SemaphoreType.DMA((3,)),
            pltpu.SemaphoreType.DMA((3,)),
            pltpu.SemaphoreType.DMA((2, 2, messages)),
            pltpu.SemaphoreType.DMA((2, 2, messages)),
            pltpu.SemaphoreType.DMA((3,)),
            pltpu.SemaphoreType.DMA((3,)),
            pltpu.SemaphoreType.DMA((length - 1,)),
            pltpu.SemaphoreType.DMA((length - 1,)),
            pltpu.SemaphoreType.DMA((2, 2, length - 1)),
            pltpu.SemaphoreType.DMA((2, 2, length - 1)),
        ],
        compiler_params=pltpu.CompilerParams(
            collective_id=0, has_side_effects=True, vmem_limit_bytes=62 * 2**20
        ),
    )(image_features, text_embed, image_head, logit_scale)
    return pl.pallas_call(
        hand_on_kernel,
        out_shape=out_shape,
        in_specs=[hbm, hbm, hbm],
        out_specs=(hbm, hbm, hbm),
        scratch_shapes=[
            pltpu.VMEM((rows, feat), bf16),
            pltpu.VMEM((rows, width), bf16),
            pltpu.VMEM((depth, width), f32),
            pltpu.SemaphoreType.DMA((2, 3)),
        ],
        compiler_params=pltpu.CompilerParams(vmem_limit_bytes=62 * 2**20),
    )(*results)


def fits_kernel(n, rows, width, depth, feat):
    pairs = n * rows
    size = 24 * pairs * rows + 4 * pairs * width + 8 * n * depth * width + 12 * rows * feat
    return (
        n % 2 == 0
        and n >= 8
        and rows % 128 == 0
        and width % (128 * CHUNKS) == 0
        and depth % 16 == 0
        and feat == n * depth
        and size <= 24 * 2**20
    )


def solution(mesh):
    n = mesh.shape["dp"]
    groups = mesh.shape["rep"] * n

    def step(image_features, text_embed, image_head, logit_scale):
        rows, width = text_embed.shape[0] // groups, text_embed.shape[1]
        depth, feat = image_head.shape[0] // groups, image_features.shape[1]
        if fits_kernel(n, rows, width, depth, feat):
            body = functools.partial(local_kernel, n)
        else:
            body = local
        split = P(("rep", "dp"), None)
        return jax.shard_map(
            body,
            mesh=mesh,
            in_specs=(split, split, split, P()),
            out_specs=(split, split, split),
            check_vma=False,
        )(image_features, text_embed, image_head, logit_scale)

    return step
```

```python
import functools

import jax
import jax.numpy as jnp
from jax import lax
from jax.experimental import pallas as pl
from jax.experimental.pallas import tpu as pltpu
from jax.sharding import PartitionSpec as P


def unit_rows(embedding):
    inv_norm = lax.rsqrt(jnp.sum(embedding * embedding, axis=1, keepdims=True) + 1e-06)
    return (embedding * inv_norm, inv_norm)


def norm_backward(embedding, inv_norm, upstream):
    inner = jnp.sum(embedding * upstream, axis=1, keepdims=True)
    return (inv_norm * upstream - embedding * (inv_norm * inv_norm * inv_norm) * inner).astype(
        jnp.bfloat16
    )


def tile_logits(logit_mult, left_rows, right_rows):
    product = lax.dot_general(
        left_rows, right_rows, (((1,), (1,)), ((), ())), preferred_element_type=jnp.float32
    )
    return logit_mult * product


def pair_coef(logits, left_lse, right_lse, left_ids, right_ids):
    label = (left_ids[:, None] == right_ids[None, :]).astype(jnp.float32)
    values = (
        jnp.exp(logits - left_lse[:, None]) + jnp.exp(logits - right_lse[None, :]) - 2.0 * label
    )
    return values.astype(jnp.bfloat16)


def local(image_features, text_embed, image_head, logit_scale):
    logit_mult = logit_scale[0]
    row_count = image_features.shape[0]
    own_ids = lax.axis_index("dp") * row_count + jnp.arange(row_count, dtype=jnp.int32)
    head_full = lax.all_gather(image_head, "dp", axis=0, tiled=True)
    img_emb = jnp.dot(image_features, head_full, preferred_element_type=jnp.float32)
    img_scaled, img_inv = unit_rows(img_emb)
    img_unit = img_scaled.astype(jnp.bfloat16)
    txt_emb = text_embed.astype(jnp.float32)
    txt_scaled, txt_inv = unit_rows(txt_emb)
    txt_unit = txt_scaled.astype(jnp.bfloat16)
    exp_tile = jnp.exp(
        tile_logits(logit_mult, img_unit, lax.all_gather(txt_unit, "dp", axis=0, tiled=True))
    )
    col_part = jnp.sum(exp_tile, axis=0)
    row_sum, col_part = (jnp.sum(exp_tile, axis=1), col_part)
    row_lse = jnp.log(row_sum)
    col_lse = jnp.log(lax.psum_scatter(col_part, "dp", scatter_dimension=0, tiled=True))
    row_all, col_all = (
        lax.all_gather(row_lse, "dp", axis=0, tiled=True),
        lax.all_gather(col_lse, "dp", axis=0, tiled=True),
    )
    img_piece = lax.all_gather(img_unit, "dp", axis=0, tiled=True)
    txt_piece = lax.all_gather(txt_unit, "dp", axis=0, tiled=True)
    count = img_piece.shape[0]
    piece_ids = jnp.arange(count, dtype=jnp.int32)
    img_coef = pair_coef(
        tile_logits(logit_mult, img_unit, txt_piece), row_lse, col_all, own_ids, piece_ids
    )
    txt_coef = pair_coef(
        tile_logits(logit_mult, txt_unit, img_piece), col_lse, row_all, own_ids, piece_ids
    )
    img_acc = jnp.dot(img_coef, txt_piece, preferred_element_type=jnp.float32)
    txt_acc = jnp.dot(txt_coef, img_piece, preferred_element_type=jnp.float32)
    img_unit_grad = logit_mult * img_acc
    txt_unit_grad = logit_mult * txt_acc
    img_emb_grad = norm_backward(img_emb, img_inv, img_unit_grad)
    text_embed_grad = norm_backward(txt_emb, txt_inv, txt_unit_grad)
    image_features_grad = lax.dot_general(
        img_emb_grad, head_full, (((1,), (1,)), ((), ())), preferred_element_type=jnp.float32
    ).astype(jnp.bfloat16)
    head_partial = lax.dot_general(
        image_features, img_emb_grad, (((0,), (0,)), ((), ())), preferred_element_type=jnp.float32
    )
    image_head_grad = lax.psum_scatter(
        head_partial.astype(jnp.bfloat16), "dp", scatter_dimension=0, tiled=True
    ).astype(jnp.float32)
    return (image_features_grad, text_embed_grad, image_head_grad)


MESH = pl.DeviceIdType.MESH
CHUNKS = 2
HEAD, GRAD = range(2)
IMAGES, IMAGE_GRADS, ROW_SUMS = range(3)
ROWS_ROWS = (((1,), (1,)), ((), ()))
COLS_COLS = (((0,), (0,)), ((), ()))


def place_of(index, n):
    depth, side = lax.div(index, 2), lax.rem(index, 2)
    return depth + side * (n - 1 - 2 * depth)


def index_at(place, n):
    place = lax.rem(place + 2 * n, n)
    side = lax.div(place, n // 2)
    return 2 * (place + side * (n - 1 - 2 * place)) + side


def step_kernel(
    n,
    feat_hbm,
    text_hbm,
    head_hbm,
    scale_ref,
    feat_out,
    text_out,
    head_out,
    feat_grad_ref,
    text_grad_ref,
    head_grad_ref,
    head_all,
    text_col,
    images,
    feat_blocks,
    feat_t_blocks,
    feat_ref,
    text_ref,
    coefs,
    row_stats,
    col_stats,
    image_out,
    image_in,
    text_part,
    text_going,
    text_coming,
    outgoing,
    incoming,
    load_sem,
    store_sem,
    send_sem,
    recv_sem,
    pair_send_sem,
    pair_recv_sem,
    stats_send_sem,
    stats_recv_sem,
    chain_send_sem,
    chain_recv_sem,
):
    rows, width = text_hbm.shape
    depth = head_hbm.shape[0]
    chunk = width // CHUNKS
    length = n // 2
    messages = CHUNKS * (n - 1) // 2
    me = lax.axis_index("dp")
    place = place_of(me, n)
    level, side = lax.div(me, 2), lax.rem(me, 2)
    other = me + 1 - 2 * side
    partner = {+1: index_at(place + 1, n), -1: index_at(place - 1, n)}

    own_head = pl.ds(pl.multiple_of(me * depth, 16), depth)
    loads = [
        pltpu.make_async_copy(head_hbm, head_all.at[own_head, :], load_sem.at[2]),
        pltpu.make_async_copy(text_hbm, text_ref, load_sem.at[0]),
        pltpu.make_async_copy(feat_hbm, feat_ref, load_sem.at[1]),
    ]
    stores = [
        pltpu.make_async_copy(feat_grad_ref, feat_out, store_sem.at[0]),
        pltpu.make_async_copy(text_grad_ref, text_out, store_sem.at[1]),
        pltpu.make_async_copy(head_grad_ref, head_out, store_sem.at[2]),
    ]
    for load in loads:
        load.start()
    barrier = pltpu.get_barrier_semaphore()
    for k in range(1, n):
        pl.semaphore_signal(
            barrier, inc=1, device_id={"dp": lax.rem(me + k, n)}, device_id_type=MESH
        )
    loads[0].wait()
    pl.semaphore_wait(barrier, n - 1)

    def columns(way, m):
        return pl.ds((m % CHUNKS + (0 if way == 1 else CHUNKS // 2)) % CHUNKS * chunk, chunk)

    def remote(kind, way, m, src, dst):
        side = 0 if way == 1 else 1
        return pltpu.make_async_remote_copy(
            src_ref=src,
            dst_ref=dst,
            send_sem=send_sem.at[kind, side, m],
            recv_sem=recv_sem.at[kind, side, m],
            device_id={"dp": partner[way]},
            device_id_type=MESH,
        )

    gathered = {HEAD: (head_all, depth)}

    def gather_copy(kind, way, m, origin_shift):
        buf, block = gathered[kind]
        owner = index_at(place - way * origin_shift, n)
        at = pl.ds(pl.multiple_of(owner * block, 16), block)
        ref = buf.at[at, columns(way, m)]
        return remote(kind, way, m, ref, ref)

    def gather_send(kind, step):
        for m in range(step * CHUNKS, min((step + 1) * CHUNKS, messages)):
            for way in (1, -1):
                if step >= 1:
                    gather_copy(kind, way, m - CHUNKS, step).wait_recv()
                gather_copy(kind, way, m, step).start()

    def gather_last(kind):
        for m in range(messages - CHUNKS, messages):
            for way in (1, -1):
                gather_copy(kind, way, m, m // CHUNKS + 1).wait_recv()

    def along(way):
        return level if way == 1 else length - 1 - level

    def chain_copy(kind, way, slot, src, dst):
        return pltpu.make_async_remote_copy(
            src_ref=src,
            dst_ref=dst,
            send_sem=chain_send_sem.at[kind, 0 if way == 1 else 1, slot],
            recv_sem=chain_recv_sem.at[kind, 0 if way == 1 else 1, slot],
            device_id={"dp": lax.rem(me + 2 * way + n, n)},
            device_id_type=MESH,
        )

    def text_copy(way, slot, shift):
        owner = level - way * shift
        ref = text_col.at[pl.ds(pl.multiple_of(owner * rows, 16), rows), :]
        return chain_copy(0, way, slot, ref, ref)

    def text_slot(slot):
        for way in (1, -1):
            if slot >= 1:

                @pl.when(along(way) >= slot)
                def _():
                    text_copy(way, slot - 1, slot).wait_recv()

            if slot <= length - 2:

                @pl.when((along(way) >= slot) & (along(way) < length - 1))
                def _():
                    text_copy(way, slot, slot).start()

    def pair_copy(kind, src, dst):
        return pltpu.make_async_remote_copy(
            src_ref=src,
            dst_ref=dst,
            send_sem=pair_send_sem.at[kind],
            recv_sem=pair_recv_sem.at[kind],
            device_id={"dp": other},
            device_id_type=MESH,
        )

    own_images = pl.ds(pl.multiple_of(side * rows, 16), rows)
    other_images = pl.ds(pl.multiple_of((1 - side) * rows, 16), rows)
    images_copy = pair_copy(IMAGES, images.at[own_images, :], images.at[own_images, :])
    images_landed = pair_copy(IMAGES, images.at[other_images, :], images.at[other_images, :])
    grads_copy = pair_copy(IMAGE_GRADS, image_out, image_in)
    sums_copy = pair_copy(ROW_SUMS, row_stats.at[side], row_stats.at[side])
    sums_landed = pair_copy(ROW_SUMS, row_stats.at[1 - side], row_stats.at[1 - side])

    gather_send(HEAD, 0)

    loads[1].wait()
    txt_emb = text_ref[...].astype(jnp.float32)
    txt_scaled, txt_inv = unit_rows(txt_emb)
    text_col[pl.ds(pl.multiple_of(level * rows, 16), rows), :] = txt_scaled.astype(jnp.bfloat16)
    text_slot(0)
    loads[2].wait()
    feat_t = feat_ref[...].astype(jnp.float32).T
    for b in range(n):
        block = feat_t[b * depth : (b + 1) * depth]
        feat_t_blocks[b] = block.astype(jnp.bfloat16)
        feat_blocks[b] = block.T.astype(jnp.bfloat16)

    def emb_part(owner):
        at = pl.ds(pl.multiple_of(owner * depth, 16), depth)
        block = feat_blocks[owner]
        return jnp.dot(block, head_all[at, :], preferred_element_type=jnp.float32)

    def emb_parts(shift):
        return emb_part(index_at(place - shift, n)) + emb_part(index_at(place + shift, n))

    img_emb = None
    for step in range(1, length):
        gather_send(HEAD, step)
        if step < length - 1:
            text_slot(step)
        part = emb_parts(step - 1) if step > 1 else emb_part(me)
        img_emb = part if img_emb is None else img_emb + part
    gather_last(HEAD)
    img_emb += emb_parts(length - 1)
    img_emb += emb_part(index_at(place + length, n))
    img_scaled, img_inv = unit_rows(img_emb)
    img_unit = img_scaled.astype(jnp.bfloat16)
    images[own_images, :] = img_unit
    images_copy.start()
    text_slot(length - 1)

    scale = scale_ref[0]
    own_exp = jnp.exp(tile_logits(scale, img_unit, text_col[...]))
    images_landed.wait_recv()
    other_exp = jnp.exp(tile_logits(scale, images[other_images, :], text_col[...]))
    exp_tile = jnp.concatenate(
        [jnp.where(side == 0, own_exp, other_exp), jnp.where(side == 0, other_exp, own_exp)], axis=0
    )
    row_part = jnp.sum(exp_tile, axis=1, keepdims=True)
    row_stats[side] = jnp.broadcast_to(row_part, (2 * rows, rows)).T[0:1, :]
    col_stats[level] = jnp.sum(exp_tile, axis=0, keepdims=True)

    def stats_copy(k, sender):
        return pltpu.make_async_remote_copy(
            src_ref=col_stats.at[sender],
            dst_ref=col_stats.at[sender],
            send_sem=stats_send_sem.at[k - 1],
            recv_sem=stats_recv_sem.at[k - 1],
            device_id={"dp": 2 * lax.rem(level + k, length) + side},
            device_id_type=MESH,
        )

    for k in range(1, length):
        stats_copy(k, level).start()
    sums_copy.start()
    sums_landed.wait_recv()
    inv_row = 1.0 / jnp.broadcast_to(row_stats[0] + row_stats[1], (rows, 2 * rows)).T[:, 0:1]
    tile = (2 * rows, length * rows)
    row_ids = lax.broadcasted_iota(jnp.int32, tile, 0) - side * rows
    col_ids = lax.broadcasted_iota(jnp.int32, tile, 1) - level * rows
    label = (row_ids == col_ids) & (row_ids >= 0) & (row_ids < rows)
    minus = jnp.where(label, 2.0, 0.0)
    for k in range(1, length):
        stats_copy(k, lax.rem(level - k + length, length)).wait_recv()
    col_sum = col_stats[0]
    for k in range(1, length):
        col_sum += col_stats[k]
    coefs[...] = (exp_tile * (inv_row + 1.0 / col_sum) - minus).astype(jnp.bfloat16)

    image_out[...] = jnp.dot(
        coefs[other_images, :], text_col[...], preferred_element_type=jnp.float32
    ).astype(jnp.bfloat16)
    grads_copy.start()
    text_acc = lax.dot_general(
        coefs[...], images[...], COLS_COLS, preferred_element_type=jnp.float32
    )
    for b in range(length):
        text_part[b] = text_acc[b * rows : (b + 1) * rows]

    def text_grad_copy(way, slot):
        which = 0 if way == 1 else 1
        return chain_copy(1, way, slot, text_going.at[which, slot], text_coming.at[which, slot])

    def text_grad_slot(slot):
        for way in (1, -1):
            which = 0 if way == 1 else 1

            @pl.when(along(way) <= slot)
            def _():
                ahead = length - 1 - slot + along(way)
                value = text_part[ahead if way == 1 else length - 1 - ahead]
                text_going[which, slot] = value.astype(jnp.bfloat16)

            if slot >= 1:

                @pl.when((along(way) <= slot) & (along(way) >= 1))
                def _():
                    ahead = length - 1 - slot + along(way)
                    value = text_part[ahead if way == 1 else length - 1 - ahead]
                    text_grad_copy(way, slot - 1).wait_recv()
                    value += text_coming[which, slot - 1].astype(jnp.float32)
                    text_going[which, slot] = value.astype(jnp.bfloat16)

            @pl.when(along(way) <= slot)
            def _():
                text_grad_copy(way, slot).start()

    text_grad_slot(0)
    img_acc = jnp.dot(
        coefs[own_images, :], text_col[...], preferred_element_type=jnp.float32
    )
    grads_copy.wait_recv()
    img_acc += image_in[...].astype(jnp.float32)
    img_emb_grad = norm_backward(img_emb, img_inv, scale * img_acc)

    def head_part(owner, cols):
        return jnp.dot(
            feat_t_blocks[owner],
            img_emb_grad[:, cols.start : cols.start + cols.size],
            preferred_element_type=jnp.float32,
        )

    def grad_copy(way, m):
        side = 0 if way == 1 else 1
        return remote(GRAD, way, m, outgoing.at[side, m], incoming.at[side, m])

    def grad_send(step):
        for m in range(step * CHUNKS, min((step + 1) * CHUNKS, messages)):
            far = length - step - (0 if m % CHUNKS < CHUNKS // 2 else 1)
            for way in (1, -1):
                side = 0 if way == 1 else 1
                value = head_part(index_at(place + way * far, n), columns(way, m))
                if step >= 1:
                    grad_copy(way, m - CHUNKS).wait_recv()
                    value += incoming[side, m - CHUNKS].astype(jnp.float32)
                outgoing[side, m] = value.astype(jnp.bfloat16)
                grad_copy(way, m).start()

    def text_side():
        for way in (1, -1):
            which = 0 if way == 1 else 1

            @pl.when(along(way) >= 1)
            def _():
                text_grad_copy(way, length - 2).wait_recv()
                text_part[level] += text_coming[which, length - 2].astype(jnp.float32)

        text_grad_ref[...] = norm_backward(txt_emb, txt_inv, scale * text_part[level])
        stores[1].start()

    def feat_side():
        feat_grad_ref[...] = lax.dot_general(
            img_emb_grad, head_all[...], ROWS_ROWS, preferred_element_type=jnp.float32
        ).astype(jnp.bfloat16)
        stores[0].start()

    for step in range(length):
        grad_send(step)
        if 1 <= step <= length - 2:
            text_grad_slot(step)
    feat_side()
    text_side()

    total = head_part(me, pl.ds(0, width))
    arrived = {0: [None] * CHUNKS, 1: [None] * CHUNKS}
    for m in range(messages - CHUNKS, messages):
        for way in (1, -1):
            grad_copy(way, m).wait_recv()
            which = 0 if way == 1 else 1
            arrived[which][columns(way, m).start // chunk] = incoming[which, m].astype(jnp.float32)
    head_grad_ref[...] = (
        total + jnp.concatenate(arrived[0], axis=1) + jnp.concatenate(arrived[1], axis=1)
    )
    stores[2].start()

    for m in range(messages):
        for way in (1, -1):
            for kind in gathered:
                gather_copy(kind, way, m, m // 2).wait_send()
            grad_copy(way, m).wait_send()
    for k in range(1, length):
        stats_copy(k, level).wait_send()
    images_copy.wait_send()
    grads_copy.wait_send()
    sums_copy.wait_send()
    for way in (1, -1):
        for slot in range(length - 1):

            @pl.when((along(way) >= slot) & (along(way) < length - 1))
            def _():
                text_copy(way, slot, slot).wait_send()

            @pl.when(along(way) <= slot)
            def _():
                text_grad_copy(way, slot).wait_send()

    for store in stores:
        store.wait()


def hand_on_kernel(*refs):
    sources, results, held, sem = refs[:3], refs[3:6], refs[6:9], refs[9]
    loads = [pltpu.make_async_copy(sources[i], held[i], sem.at[0, i]) for i in range(3)]
    stores = [pltpu.make_async_copy(held[i], results[i], sem.at[1, i]) for i in range(3)]
    for load in loads:
        load.start()
    for load, store in zip(loads, stores):
        load.wait()
        store.start()
    for store in stores:
        store.wait()


def local_kernel(n, image_features, text_embed, image_head, logit_scale):
    rows, width = text_embed.shape
    depth, feat = image_head.shape[0], image_features.shape[1]
    length = n // 2
    chunk = width // CHUNKS
    messages = CHUNKS * (n - 1) // 2
    bf16, f32 = jnp.bfloat16, jnp.float32
    hbm = pl.BlockSpec(memory_space=pltpu.HBM)
    out_shape = (
        jax.ShapeDtypeStruct((rows, feat), bf16),
        jax.ShapeDtypeStruct((rows, width), bf16),
        jax.ShapeDtypeStruct((depth, width), f32),
    )
    results = pl.pallas_call(
        functools.partial(step_kernel, n),
        out_shape=out_shape,
        in_specs=[hbm, hbm, hbm, pl.BlockSpec(memory_space=pltpu.SMEM)],
        out_specs=(hbm, hbm, hbm),
        scratch_shapes=[
            pltpu.VMEM((rows, feat), bf16),
            pltpu.VMEM((rows, width), bf16),
            pltpu.VMEM((depth, width), f32),
            pltpu.VMEM((n * depth, width), bf16),
            pltpu.VMEM((length * rows, width), bf16),
            pltpu.VMEM((2 * rows, width), bf16),
            pltpu.VMEM((n, rows, depth), bf16),
            pltpu.VMEM((n, depth, rows), bf16),
            pltpu.VMEM((rows, feat), bf16),
            pltpu.VMEM((rows, width), bf16),
            pltpu.VMEM((2 * rows, length * rows), bf16),
            pltpu.VMEM((2, 1, 2 * rows), f32),
            pltpu.VMEM((length, 1, length * rows), f32),
            pltpu.VMEM((rows, width), bf16),
            pltpu.VMEM((rows, width), bf16),
            pltpu.VMEM((length, rows, width), f32),
            pltpu.VMEM((2, length - 1, rows, width), bf16),
            pltpu.VMEM((2, length - 1, rows, width), bf16),
            pltpu.VMEM((2, messages, depth, chunk), bf16),
            pltpu.VMEM((2, messages, depth, chunk), bf16),
            pltpu.SemaphoreType.DMA((3,)),
            pltpu.SemaphoreType.DMA((3,)),
            pltpu.SemaphoreType.DMA((2, 2, messages)),
            pltpu.SemaphoreType.DMA((2, 2, messages)),
            pltpu.SemaphoreType.DMA((3,)),
            pltpu.SemaphoreType.DMA((3,)),
            pltpu.SemaphoreType.DMA((length - 1,)),
            pltpu.SemaphoreType.DMA((length - 1,)),
            pltpu.SemaphoreType.DMA((2, 2, length - 1)),
            pltpu.SemaphoreType.DMA((2, 2, length - 1)),
        ],
        compiler_params=pltpu.CompilerParams(
            collective_id=0, has_side_effects=True, vmem_limit_bytes=62 * 2**20
        ),
    )(image_features, text_embed, image_head, logit_scale)
    return pl.pallas_call(
        hand_on_kernel,
        out_shape=out_shape,
        in_specs=[hbm, hbm, hbm],
        out_specs=(hbm, hbm, hbm),
        scratch_shapes=[
            pltpu.VMEM((rows, feat), bf16),
            pltpu.VMEM((rows, width), bf16),
            pltpu.VMEM((depth, width), f32),
            pltpu.SemaphoreType.DMA((2, 3)),
        ],
        compiler_params=pltpu.CompilerParams(vmem_limit_bytes=62 * 2**20),
    )(*results)


def fits_kernel(n, rows, width, depth, feat):
    pairs = n * rows
    size = 24 * pairs * rows + 4 * pairs * width + 8 * n * depth * width + 12 * rows * feat
    return (
        n % 2 == 0
        and n >= 8
        and rows % 128 == 0
        and width % (128 * CHUNKS) == 0
        and depth % 16 == 0
        and feat == n * depth
        and size <= 24 * 2**20
    )


def solution(mesh):
    n = mesh.shape["dp"]
    groups = mesh.shape["rep"] * n

    def step(image_features, text_embed, image_head, logit_scale):
        rows, width = text_embed.shape[0] // groups, text_embed.shape[1]
        depth, feat = image_head.shape[0] // groups, image_features.shape[1]
        if fits_kernel(n, rows, width, depth, feat):
            body = functools.partial(local_kernel, n)
        else:
            body = local
        split = P(("rep", "dp"), None)
        return jax.shard_map(
            body,
            mesh=mesh,
            in_specs=(split, split, split, P()),
            out_specs=(split, split, split),
            check_vma=False,
        )(image_features, text_embed, image_head, logit_scale)

    return step
```

```python
import functools

import jax
import jax.numpy as jnp
from jax import lax
from jax.experimental import pallas as pl
from jax.experimental.pallas import tpu as pltpu
from jax.sharding import PartitionSpec as P


def unit_rows(embedding):
    inv_norm = lax.rsqrt(jnp.sum(embedding * embedding, axis=1, keepdims=True) + 1e-06)
    return (embedding * inv_norm, inv_norm)


def norm_backward(embedding, inv_norm, upstream):
    inner = jnp.sum(embedding * upstream, axis=1, keepdims=True)
    return (inv_norm * upstream - embedding * (inv_norm * inv_norm * inv_norm) * inner).astype(
        jnp.bfloat16
    )


def tile_logits(logit_mult, left_rows, right_rows):
    product = lax.dot_general(
        left_rows, right_rows, (((1,), (1,)), ((), ())), preferred_element_type=jnp.float32
    )
    return logit_mult * product


def pair_coef(logits, left_lse, right_lse, left_ids, right_ids):
    label = (left_ids[:, None] == right_ids[None, :]).astype(jnp.float32)
    values = (
        jnp.exp(logits - left_lse[:, None]) + jnp.exp(logits - right_lse[None, :]) - 2.0 * label
    )
    return values.astype(jnp.bfloat16)


def local(image_features, text_embed, image_head, logit_scale):
    logit_mult = logit_scale[0]
    row_count = image_features.shape[0]
    own_ids = lax.axis_index("dp") * row_count + jnp.arange(row_count, dtype=jnp.int32)
    head_full = lax.all_gather(image_head, "dp", axis=0, tiled=True)
    img_emb = jnp.dot(image_features, head_full, preferred_element_type=jnp.float32)
    img_scaled, img_inv = unit_rows(img_emb)
    img_unit = img_scaled.astype(jnp.bfloat16)
    txt_emb = text_embed.astype(jnp.float32)
    txt_scaled, txt_inv = unit_rows(txt_emb)
    txt_unit = txt_scaled.astype(jnp.bfloat16)
    exp_tile = jnp.exp(
        tile_logits(logit_mult, img_unit, lax.all_gather(txt_unit, "dp", axis=0, tiled=True))
    )
    col_part = jnp.sum(exp_tile, axis=0)
    row_sum, col_part = (jnp.sum(exp_tile, axis=1), col_part)
    row_lse = jnp.log(row_sum)
    col_lse = jnp.log(lax.psum_scatter(col_part, "dp", scatter_dimension=0, tiled=True))
    row_all, col_all = (
        lax.all_gather(row_lse, "dp", axis=0, tiled=True),
        lax.all_gather(col_lse, "dp", axis=0, tiled=True),
    )
    img_piece = lax.all_gather(img_unit, "dp", axis=0, tiled=True)
    txt_piece = lax.all_gather(txt_unit, "dp", axis=0, tiled=True)
    count = img_piece.shape[0]
    piece_ids = jnp.arange(count, dtype=jnp.int32)
    img_coef = pair_coef(
        tile_logits(logit_mult, img_unit, txt_piece), row_lse, col_all, own_ids, piece_ids
    )
    txt_coef = pair_coef(
        tile_logits(logit_mult, txt_unit, img_piece), col_lse, row_all, own_ids, piece_ids
    )
    img_acc = jnp.dot(img_coef, txt_piece, preferred_element_type=jnp.float32)
    txt_acc = jnp.dot(txt_coef, img_piece, preferred_element_type=jnp.float32)
    img_unit_grad = logit_mult * img_acc
    txt_unit_grad = logit_mult * txt_acc
    img_emb_grad = norm_backward(img_emb, img_inv, img_unit_grad)
    text_embed_grad = norm_backward(txt_emb, txt_inv, txt_unit_grad)
    image_features_grad = lax.dot_general(
        img_emb_grad, head_full, (((1,), (1,)), ((), ())), preferred_element_type=jnp.float32
    ).astype(jnp.bfloat16)
    head_partial = lax.dot_general(
        image_features, img_emb_grad, (((0,), (0,)), ((), ())), preferred_element_type=jnp.float32
    )
    image_head_grad = lax.psum_scatter(
        head_partial.astype(jnp.bfloat16), "dp", scatter_dimension=0, tiled=True
    ).astype(jnp.float32)
    return (image_features_grad, text_embed_grad, image_head_grad)


MESH = pl.DeviceIdType.MESH
HEAD, TEXT, IMAGE, GRAD = range(4)
ROWS_ROWS = (((1,), (1,)), ((), ()))


def place_of(index, n):
    depth, side = lax.div(index, 2), lax.rem(index, 2)
    return depth + side * (n - 1 - 2 * depth)


def index_at(place, n):
    place = lax.rem(place + 2 * n, n)
    side = lax.div(place, n // 2)
    return 2 * (place + side * (n - 1 - 2 * place)) + side


def step_kernel(
    n,
    feat_hbm,
    text_hbm,
    head_hbm,
    scale_ref,
    feat_out,
    text_out,
    head_out,
    feat_grad_ref,
    text_grad_ref,
    head_grad_ref,
    head_all,
    text_all,
    image_all,
    feat_blocks,
    feat_t_blocks,
    feat_ref,
    text_ref,
    exp_blocks,
    stats,
    inv_cols,
    outgoing,
    incoming,
    load_sem,
    store_sem,
    send_sem,
    recv_sem,
    stats_send_sem,
    stats_recv_sem,
):
    rows, width = text_hbm.shape
    depth = head_hbm.shape[0]
    pairs = n * rows
    half = width // 2
    messages = n - 1
    me = lax.axis_index("dp")
    place = place_of(me, n)
    partner = {+1: index_at(place + 1, n), -1: index_at(place - 1, n)}

    own_head = head_all.at[pl.ds(pl.multiple_of(me * depth, 16), depth), :]
    loads = [
        pltpu.make_async_copy(head_hbm, own_head, load_sem.at[0]),
        pltpu.make_async_copy(text_hbm, text_ref, load_sem.at[1]),
        pltpu.make_async_copy(feat_hbm, feat_ref, load_sem.at[2]),
    ]
    stores = [
        pltpu.make_async_copy(feat_grad_ref, feat_out, store_sem.at[0]),
        pltpu.make_async_copy(text_grad_ref, text_out, store_sem.at[1]),
        pltpu.make_async_copy(head_grad_ref, head_out, store_sem.at[2]),
    ]
    for load in loads:
        load.start()
    barrier = pltpu.get_barrier_semaphore()
    for k in range(1, n):
        pl.semaphore_signal(
            barrier, inc=1, device_id={"dp": lax.rem(me + k, n)}, device_id_type=MESH
        )
    loads[0].wait()
    pl.semaphore_wait(barrier, n - 1)

    def columns(way, m):
        first = (m % 2 == 0) == (way == 1)
        return pl.ds(0 if first else half, half)

    def remote(kind, way, m, src, dst):
        side = 0 if way == 1 else 1
        return pltpu.make_async_remote_copy(
            src_ref=src,
            dst_ref=dst,
            send_sem=send_sem.at[kind, side, m],
            recv_sem=recv_sem.at[kind, side, m],
            device_id={"dp": partner[way]},
            device_id_type=MESH,
        )

    gathered = {HEAD: (head_all, depth), TEXT: (text_all, rows), IMAGE: (image_all, rows)}

    def gather_copy(kind, way, m, origin_shift):
        buf, block = gathered[kind]
        owner = index_at(place - way * origin_shift, n)
        ref = buf.at[pl.ds(pl.multiple_of(owner * block, 16), block), columns(way, m)]
        return remote(kind, way, m, ref, ref)

    def gather_send(kind, m):
        for way in (1, -1):
            if m >= 2:
                gather_copy(kind, way, m - 2, m // 2).wait_recv()
            gather_copy(kind, way, m, m // 2).start()

    def gather_last(kind):
        for m in range(max(messages - 2, 0), messages):
            for way in (1, -1):
                gather_copy(kind, way, m, m // 2 + 1).wait_recv()

    gather_send(HEAD, 0)
    gather_send(HEAD, 1)

    loads[1].wait()
    txt_emb = text_ref[...].astype(jnp.float32)
    txt_scaled, txt_inv = unit_rows(txt_emb)
    text_all[pl.ds(pl.multiple_of(me * rows, 16), rows), :] = txt_scaled.astype(jnp.bfloat16)
    gather_send(HEAD, 2)
    loads[2].wait()
    feat_t = feat_ref[...].astype(jnp.float32).T
    for b in range(n):
        block = feat_t[b * depth : (b + 1) * depth]
        feat_t_blocks[b] = block.astype(jnp.bfloat16)
        feat_blocks[b] = block.T.astype(jnp.bfloat16)

    def emb_part(owner):
        return jnp.dot(
            feat_blocks[owner],
            head_all[pl.ds(pl.multiple_of(owner * depth, 16), depth), :],
            preferred_element_type=jnp.float32,
        )

    gather_send(HEAD, 3)
    img_emb = emb_part(me)
    for way in (1, -1):
        img_emb += emb_part(index_at(place - way, n))
    for m in range(4, messages):
        gather_send(HEAD, m)
        if m % 2 == 1:
            for way in (1, -1):
                img_emb += emb_part(index_at(place - way * (m // 2), n))
    gather_send(TEXT, 0)
    gather_send(TEXT, 1)
    gather_last(HEAD)
    for way in (1, -1):
        img_emb += emb_part(index_at(place - way * (n // 2 - 1), n))
    img_emb += emb_part(index_at(place + n // 2, n))
    img_scaled, img_inv = unit_rows(img_emb)
    img_unit = img_scaled.astype(jnp.bfloat16)
    image_all[pl.ds(pl.multiple_of(me * rows, 16), rows), :] = img_unit

    scale = scale_ref[0]

    def exp_block(owner):
        at = pl.ds(pl.multiple_of(owner * rows, 16), rows)
        exp_blocks[owner] = jnp.exp(tile_logits(scale, img_unit, text_all[at, :]))

    image_sent = 0
    for m in range(2, messages):
        gather_send(TEXT, m)
        if m % 2 == 0 and image_sent < 2:
            gather_send(IMAGE, image_sent)
            image_sent += 1
        if m == 2:
            exp_block(me)
        if m % 2 == 1:
            for way in (1, -1):
                exp_block(index_at(place - way * (m // 2), n))
    gather_last(TEXT)
    for way in (1, -1):
        exp_block(index_at(place - way * (n // 2 - 1), n))
    exp_block(index_at(place + n // 2, n))

    exp_rows = jnp.concatenate([exp_blocks[b] for b in range(n)], axis=1)
    row_sum = jnp.sum(exp_rows, axis=1, keepdims=True)
    stats[me, :, 0:pairs] = jnp.sum(exp_rows, axis=0, keepdims=True)
    stats[me, :, pairs : pairs + rows] = jnp.broadcast_to(row_sum, (rows, rows)).T[0:1, :]

    def stats_copy(k, sender):
        return pltpu.make_async_remote_copy(
            src_ref=stats.at[sender],
            dst_ref=stats.at[sender],
            send_sem=stats_send_sem.at[k - 1],
            recv_sem=stats_recv_sem.at[k - 1],
            device_id={"dp": lax.rem(me + k, n)},
            device_id_type=MESH,
        )

    for k in range(1, n):
        stats_copy(k, me).start()
    while image_sent < messages - 2:
        gather_send(IMAGE, image_sent)
        image_sent += 1
    for k in range(1, n):
        stats_copy(k, lax.rem(me - k + n, n)).wait_recv()

    col_sum = stats[0, :, 0:pairs]
    for b in range(1, n):
        col_sum += stats[b, :, 0:pairs]
    inv_col = 1.0 / col_sum
    inv_cols[...] = inv_col
    row_ids = lax.broadcasted_iota(jnp.int32, (rows, pairs), 0) + me * rows
    label = (row_ids == lax.broadcasted_iota(jnp.int32, (rows, pairs), 1)).astype(jnp.float32)
    img_coef = exp_rows * (1.0 / row_sum + inv_col) - 2.0 * label
    img_acc = jnp.dot(
        img_coef.astype(jnp.bfloat16), text_all[...], preferred_element_type=jnp.float32
    )
    img_emb_grad = norm_backward(img_emb, img_inv, scale * img_acc)

    def head_part(owner, cols):
        return jnp.dot(
            feat_t_blocks[owner],
            img_emb_grad[:, cols.start : cols.start + half],
            preferred_element_type=jnp.float32,
        )

    def grad_copy(way, m):
        side = 0 if way == 1 else 1
        return remote(GRAD, way, m, outgoing.at[side, m], incoming.at[side, m])

    def grad_send(m):
        for way in (1, -1):
            side = 0 if way == 1 else 1
            value = head_part(index_at(place + way * (n // 2 - (m + 1) // 2), n), columns(way, m))
            if m >= 2:
                grad_copy(way, m - 2).wait_recv()
                value += incoming[side, m - 2].astype(jnp.float32)
            outgoing[side, m] = value.astype(jnp.bfloat16)
            grad_copy(way, m).start()

    def text_side():
        own = pl.ds(pl.multiple_of(me * rows, 128), rows)
        own_text = text_all[pl.ds(pl.multiple_of(me * rows, 16), rows), :]
        exp_texts = jnp.exp(tile_logits(scale, own_text, image_all[...]))
        inv_row = 1.0 / jnp.concatenate(
            [stats[b, :, pairs : pairs + rows] for b in range(n)], axis=1
        )
        inv_own = jnp.broadcast_to(inv_cols[:, own], (rows, rows)).T[:, 0:1]
        coef = exp_texts * (inv_own + inv_row) - 2.0 * label
        acc = jnp.dot(
            coef.astype(jnp.bfloat16), image_all[...], preferred_element_type=jnp.float32
        )
        text_grad_ref[...] = norm_backward(txt_emb, txt_inv, scale * acc)
        stores[1].start()

    def feat_side():
        feat_grad_ref[...] = lax.dot_general(
            img_emb_grad, head_all[...], ROWS_ROWS, preferred_element_type=jnp.float32
        ).astype(jnp.bfloat16)
        stores[0].start()

    for m in range(messages):
        grad_send(m)
        if m >= 1 and image_sent < messages:
            gather_send(IMAGE, image_sent)
            image_sent += 1

    feat_side()
    gather_last(IMAGE)
    text_side()
    total = [head_part(me, pl.ds(0, half)), head_part(me, pl.ds(half, half))]
    for m in range(messages - 2, messages):
        for way in (1, -1):
            grad_copy(way, m).wait_recv()
            which = columns(way, m).start // half
            total[which] += incoming[0 if way == 1 else 1, m].astype(jnp.float32)
    head_grad_ref[:, 0:half] = total[0]
    head_grad_ref[:, half:width] = total[1]
    stores[2].start()

    for m in range(messages):
        for way in (1, -1):
            for kind in gathered:
                gather_copy(kind, way, m, m // 2).wait_send()
            grad_copy(way, m).wait_send()
    for k in range(1, n):
        stats_copy(k, me).wait_send()
    for store in stores:
        store.wait()


def hand_on_kernel(*refs):
    sources, results, held, sem = refs[:3], refs[3:6], refs[6:9], refs[9]
    loads = [pltpu.make_async_copy(sources[i], held[i], sem.at[0, i]) for i in range(3)]
    stores = [pltpu.make_async_copy(held[i], results[i], sem.at[1, i]) for i in range(3)]
    for load in loads:
        load.start()
    for load, store in zip(loads, stores):
        load.wait()
        store.start()
    for store in stores:
        store.wait()


def local_kernel(n, image_features, text_embed, image_head, logit_scale):
    rows, width = text_embed.shape
    depth, feat = image_head.shape[0], image_features.shape[1]
    pairs = n * rows
    half = width // 2
    bf16, f32 = jnp.bfloat16, jnp.float32
    hbm = pl.BlockSpec(memory_space=pltpu.HBM)
    out_shape = (
        jax.ShapeDtypeStruct((rows, feat), bf16),
        jax.ShapeDtypeStruct((rows, width), bf16),
        jax.ShapeDtypeStruct((depth, width), f32),
    )
    results = pl.pallas_call(
        functools.partial(step_kernel, n),
        out_shape=out_shape,
        in_specs=[hbm, hbm, hbm, pl.BlockSpec(memory_space=pltpu.SMEM)],
        out_specs=(hbm, hbm, hbm),
        scratch_shapes=[
            pltpu.VMEM((rows, feat), bf16),
            pltpu.VMEM((rows, width), bf16),
            pltpu.VMEM((depth, width), f32),
            pltpu.VMEM((n * depth, width), bf16),
            pltpu.VMEM((pairs, width), bf16),
            pltpu.VMEM((pairs, width), bf16),
            pltpu.VMEM((n, rows, depth), bf16),
            pltpu.VMEM((n, depth, rows), bf16),
            pltpu.VMEM((rows, feat), bf16),
            pltpu.VMEM((rows, width), bf16),
            pltpu.VMEM((n, rows, rows), f32),
            pltpu.VMEM((n, 1, pairs + rows), f32),
            pltpu.VMEM((1, pairs), f32),
            pltpu.VMEM((2, n - 1, depth, half), bf16),
            pltpu.VMEM((2, n - 1, depth, half), bf16),
            pltpu.SemaphoreType.DMA((3,)),
            pltpu.SemaphoreType.DMA((3,)),
            pltpu.SemaphoreType.DMA((4, 2, n - 1)),
            pltpu.SemaphoreType.DMA((4, 2, n - 1)),
            pltpu.SemaphoreType.DMA((n - 1,)),
            pltpu.SemaphoreType.DMA((n - 1,)),
        ],
        compiler_params=pltpu.CompilerParams(
            collective_id=0, has_side_effects=True, vmem_limit_bytes=62 * 2**20
        ),
    )(image_features, text_embed, image_head, logit_scale)
    return pl.pallas_call(
        hand_on_kernel,
        out_shape=out_shape,
        in_specs=[hbm, hbm, hbm],
        out_specs=(hbm, hbm, hbm),
        scratch_shapes=[
            pltpu.VMEM((rows, feat), bf16),
            pltpu.VMEM((rows, width), bf16),
            pltpu.VMEM((depth, width), f32),
            pltpu.SemaphoreType.DMA((2, 3)),
        ],
        compiler_params=pltpu.CompilerParams(vmem_limit_bytes=62 * 2**20),
    )(*results)


def fits_kernel(n, rows, width, depth, feat):
    pairs = n * rows
    size = 24 * pairs * rows + 4 * pairs * width + 8 * n * depth * width + 12 * rows * feat
    return (
        n % 2 == 0
        and n >= 8
        and rows % 128 == 0
        and width % 256 == 0
        and depth % 16 == 0
        and feat == n * depth
        and size <= 24 * 2**20
    )


def solution(mesh):
    n = mesh.shape["dp"]
    groups = mesh.shape["rep"] * n

    def step(image_features, text_embed, image_head, logit_scale):
        rows, width = text_embed.shape[0] // groups, text_embed.shape[1]
        depth, feat = image_head.shape[0] // groups, image_features.shape[1]
        if fits_kernel(n, rows, width, depth, feat):
            body = functools.partial(local_kernel, n)
        else:
            body = local
        split = P(("rep", "dp"), None)
        return jax.shard_map(
            body,
            mesh=mesh,
            in_specs=(split, split, split, P()),
            out_specs=(split, split, split),
            check_vma=False,
        )(image_features, text_embed, image_head, logit_scale)

    return step
```

```python
import functools

import jax
import jax.numpy as jnp
from jax import lax
from jax.experimental import pallas as pl
from jax.experimental.pallas import tpu as pltpu
from jax.sharding import PartitionSpec as P


def unit_rows(embedding):
    inv_norm = lax.rsqrt(jnp.sum(embedding * embedding, axis=1, keepdims=True) + 1e-06)
    return (embedding * inv_norm, inv_norm)


def norm_backward(embedding, inv_norm, upstream):
    inner = jnp.sum(embedding * upstream, axis=1, keepdims=True)
    return (inv_norm * upstream - embedding * (inv_norm * inv_norm * inv_norm) * inner).astype(
        jnp.bfloat16
    )


def tile_logits(logit_mult, left_rows, right_rows):
    product = lax.dot_general(
        left_rows, right_rows, (((1,), (1,)), ((), ())), preferred_element_type=jnp.float32
    )
    return logit_mult * product


def pair_coef(logits, left_lse, right_lse, left_ids, right_ids):
    label = (left_ids[:, None] == right_ids[None, :]).astype(jnp.float32)
    values = (
        jnp.exp(logits - left_lse[:, None]) + jnp.exp(logits - right_lse[None, :]) - 2.0 * label
    )
    return values.astype(jnp.bfloat16)


def local(image_features, text_embed, image_head, logit_scale):
    logit_mult = logit_scale[0]
    row_count = image_features.shape[0]
    own_ids = lax.axis_index("dp") * row_count + jnp.arange(row_count, dtype=jnp.int32)
    head_full = lax.all_gather(image_head, "dp", axis=0, tiled=True)
    img_emb = jnp.dot(image_features, head_full, preferred_element_type=jnp.float32)
    img_scaled, img_inv = unit_rows(img_emb)
    img_unit = img_scaled.astype(jnp.bfloat16)
    txt_emb = text_embed.astype(jnp.float32)
    txt_scaled, txt_inv = unit_rows(txt_emb)
    txt_unit = txt_scaled.astype(jnp.bfloat16)
    exp_tile = jnp.exp(
        tile_logits(logit_mult, img_unit, lax.all_gather(txt_unit, "dp", axis=0, tiled=True))
    )
    col_part = jnp.sum(exp_tile, axis=0)
    row_sum, col_part = (jnp.sum(exp_tile, axis=1), col_part)
    row_lse = jnp.log(row_sum)
    col_lse = jnp.log(lax.psum_scatter(col_part, "dp", scatter_dimension=0, tiled=True))
    row_all, col_all = (
        lax.all_gather(row_lse, "dp", axis=0, tiled=True),
        lax.all_gather(col_lse, "dp", axis=0, tiled=True),
    )
    img_piece = lax.all_gather(img_unit, "dp", axis=0, tiled=True)
    txt_piece = lax.all_gather(txt_unit, "dp", axis=0, tiled=True)
    count = img_piece.shape[0]
    piece_ids = jnp.arange(count, dtype=jnp.int32)
    img_coef = pair_coef(
        tile_logits(logit_mult, img_unit, txt_piece), row_lse, col_all, own_ids, piece_ids
    )
    txt_coef = pair_coef(
        tile_logits(logit_mult, txt_unit, img_piece), col_lse, row_all, own_ids, piece_ids
    )
    img_acc = jnp.dot(img_coef, txt_piece, preferred_element_type=jnp.float32)
    txt_acc = jnp.dot(txt_coef, img_piece, preferred_element_type=jnp.float32)
    img_unit_grad = logit_mult * img_acc
    txt_unit_grad = logit_mult * txt_acc
    img_emb_grad = norm_backward(img_emb, img_inv, img_unit_grad)
    text_embed_grad = norm_backward(txt_emb, txt_inv, txt_unit_grad)
    image_features_grad = lax.dot_general(
        img_emb_grad, head_full, (((1,), (1,)), ((), ())), preferred_element_type=jnp.float32
    ).astype(jnp.bfloat16)
    head_partial = lax.dot_general(
        image_features, img_emb_grad, (((0,), (0,)), ((), ())), preferred_element_type=jnp.float32
    )
    image_head_grad = lax.psum_scatter(
        head_partial.astype(jnp.bfloat16), "dp", scatter_dimension=0, tiled=True
    ).astype(jnp.float32)
    return (image_features_grad, text_embed_grad, image_head_grad)


MESH = pl.DeviceIdType.MESH
HEAD, TEXT, IMAGE, GRAD = range(4)
ROWS_ROWS = (((1,), (1,)), ((), ()))


def place_of(index, n):
    depth, side = lax.div(index, 2), lax.rem(index, 2)
    return depth + side * (n - 1 - 2 * depth)


def index_at(place, n):
    place = lax.rem(place + 2 * n, n)
    side = lax.div(place, n // 2)
    return 2 * (place + side * (n - 1 - 2 * place)) + side


def step_kernel(
    n,
    feat_hbm,
    text_hbm,
    head_hbm,
    scale_ref,
    feat_out,
    text_out,
    head_out,
    feat_grad_ref,
    text_grad_ref,
    head_grad_ref,
    head_all,
    text_all,
    image_all,
    feat_blocks,
    feat_t_blocks,
    feat_ref,
    text_ref,
    exp_blocks,
    stats,
    inv_cols,
    outgoing,
    incoming,
    load_sem,
    store_sem,
    send_sem,
    recv_sem,
    stats_send_sem,
    stats_recv_sem,
):
    rows, width = text_hbm.shape
    depth = head_hbm.shape[0]
    pairs = n * rows
    half = width // 2
    messages = n - 1
    me = lax.axis_index("dp")
    place = place_of(me, n)
    partner = {+1: index_at(place + 1, n), -1: index_at(place - 1, n)}

    own_head = head_all.at[pl.ds(pl.multiple_of(me * depth, 16), depth), :]
    loads = [
        pltpu.make_async_copy(head_hbm, own_head, load_sem.at[0]),
        pltpu.make_async_copy(text_hbm, text_ref, load_sem.at[1]),
        pltpu.make_async_copy(feat_hbm, feat_ref, load_sem.at[2]),
    ]
    stores = [
        pltpu.make_async_copy(feat_grad_ref, feat_out, store_sem.at[0]),
        pltpu.make_async_copy(text_grad_ref, text_out, store_sem.at[1]),
        pltpu.make_async_copy(head_grad_ref, head_out, store_sem.at[2]),
    ]
    for load in loads:
        load.start()
    barrier = pltpu.get_barrier_semaphore()
    for k in range(1, n):
        pl.semaphore_signal(
            barrier, inc=1, device_id={"dp": lax.rem(me + k, n)}, device_id_type=MESH
        )
    loads[0].wait()
    pl.semaphore_wait(barrier, n - 1)

    def columns(way, m):
        first = (m % 2 == 0) == (way == 1)
        return pl.ds(0 if first else half, half)

    def remote(kind, way, m, src, dst):
        side = 0 if way == 1 else 1
        return pltpu.make_async_remote_copy(
            src_ref=src,
            dst_ref=dst,
            send_sem=send_sem.at[kind, side, m],
            recv_sem=recv_sem.at[kind, side, m],
            device_id={"dp": partner[way]},
            device_id_type=MESH,
        )

    gathered = {HEAD: (head_all, depth), TEXT: (text_all, rows), IMAGE: (image_all, rows)}

    def gather_copy(kind, way, m, origin_shift):
        buf, block = gathered[kind]
        owner = index_at(place - way * origin_shift, n)
        ref = buf.at[pl.ds(pl.multiple_of(owner * block, 16), block), columns(way, m)]
        return remote(kind, way, m, ref, ref)

    def gather_send(kind, m):
        for way in (1, -1):
            if m >= 2:
                gather_copy(kind, way, m - 2, m // 2).wait_recv()
            gather_copy(kind, way, m, m // 2).start()

    def gather_last(kind):
        for m in range(max(messages - 2, 0), messages):
            for way in (1, -1):
                gather_copy(kind, way, m, m // 2 + 1).wait_recv()

    gather_send(HEAD, 0)
    gather_send(HEAD, 1)

    loads[1].wait()
    txt_emb = text_ref[...].astype(jnp.float32)
    txt_scaled, txt_inv = unit_rows(txt_emb)
    text_all[pl.ds(pl.multiple_of(me * rows, 16), rows), :] = txt_scaled.astype(jnp.bfloat16)
    gather_send(HEAD, 2)
    loads[2].wait()
    feat_t = feat_ref[...].astype(jnp.float32).T
    for b in range(n):
        block = feat_t[b * depth : (b + 1) * depth]
        feat_t_blocks[b] = block.astype(jnp.bfloat16)
        feat_blocks[b] = block.T.astype(jnp.bfloat16)

    def emb_part(owner):
        return jnp.dot(
            feat_blocks[owner],
            head_all[pl.ds(pl.multiple_of(owner * depth, 16), depth), :],
            preferred_element_type=jnp.float32,
        )

    gather_send(HEAD, 3)
    img_emb = emb_part(me)
    for way in (1, -1):
        img_emb += emb_part(index_at(place - way, n))
    for m in range(4, messages):
        gather_send(HEAD, m)
        if m % 2 == 1:
            for way in (1, -1):
                img_emb += emb_part(index_at(place - way * (m // 2), n))
    gather_send(TEXT, 0)
    gather_send(TEXT, 1)
    gather_last(HEAD)
    for way in (1, -1):
        img_emb += emb_part(index_at(place - way * (n // 2 - 1), n))
    img_emb += emb_part(index_at(place + n // 2, n))
    img_scaled, img_inv = unit_rows(img_emb)
    img_unit = img_scaled.astype(jnp.bfloat16)
    image_all[pl.ds(pl.multiple_of(me * rows, 16), rows), :] = img_unit

    scale = scale_ref[0]

    def exp_block(owner):
        at = pl.ds(pl.multiple_of(owner * rows, 16), rows)
        exp_blocks[owner] = jnp.exp(tile_logits(scale, img_unit, text_all[at, :]))

    image_sent = 0
    for m in range(2, messages):
        gather_send(TEXT, m)
        if m % 2 == 0 and image_sent < 2:
            gather_send(IMAGE, image_sent)
            image_sent += 1
        if m == 2:
            exp_block(me)
        if m % 2 == 1:
            for way in (1, -1):
                exp_block(index_at(place - way * (m // 2), n))
    gather_last(TEXT)
    for way in (1, -1):
        exp_block(index_at(place - way * (n // 2 - 1), n))
    exp_block(index_at(place + n // 2, n))

    exp_rows = jnp.concatenate([exp_blocks[b] for b in range(n)], axis=1)
    row_sum = jnp.sum(exp_rows, axis=1, keepdims=True)
    stats[me, :, 0:pairs] = jnp.sum(exp_rows, axis=0, keepdims=True)
    stats[me, :, pairs : pairs + rows] = jnp.broadcast_to(row_sum, (rows, rows)).T[0:1, :]

    def stats_copy(k, sender):
        return pltpu.make_async_remote_copy(
            src_ref=stats.at[sender],
            dst_ref=stats.at[sender],
            send_sem=stats_send_sem.at[k - 1],
            recv_sem=stats_recv_sem.at[k - 1],
            device_id={"dp": lax.rem(me + k, n)},
            device_id_type=MESH,
        )

    for k in range(1, n):
        stats_copy(k, me).start()
    while image_sent < messages - 2:
        gather_send(IMAGE, image_sent)
        image_sent += 1
    for k in range(1, n):
        stats_copy(k, lax.rem(me - k + n, n)).wait_recv()

    col_sum = stats[0, :, 0:pairs]
    for b in range(1, n):
        col_sum += stats[b, :, 0:pairs]
    inv_col = 1.0 / col_sum
    inv_cols[...] = inv_col
    row_ids = lax.broadcasted_iota(jnp.int32, (rows, pairs), 0) + me * rows
    label = (row_ids == lax.broadcasted_iota(jnp.int32, (rows, pairs), 1)).astype(jnp.float32)
    img_coef = exp_rows * (1.0 / row_sum + inv_col) - 2.0 * label
    img_acc = jnp.dot(
        img_coef.astype(jnp.bfloat16), text_all[...], preferred_element_type=jnp.float32
    )
    img_emb_grad = norm_backward(img_emb, img_inv, scale * img_acc)

    def head_part(owner, cols):
        return jnp.dot(
            feat_t_blocks[owner],
            img_emb_grad[:, cols.start : cols.start + half],
            preferred_element_type=jnp.float32,
        )

    def grad_copy(way, m):
        side = 0 if way == 1 else 1
        return remote(GRAD, way, m, outgoing.at[side, m], incoming.at[side, m])

    def grad_send(m):
        for way in (1, -1):
            side = 0 if way == 1 else 1
            value = head_part(index_at(place + way * (n // 2 - (m + 1) // 2), n), columns(way, m))
            if m >= 2:
                grad_copy(way, m - 2).wait_recv()
                value += incoming[side, m - 2].astype(jnp.float32)
            outgoing[side, m] = value.astype(jnp.bfloat16)
            grad_copy(way, m).start()

    def text_side():
        own = pl.ds(pl.multiple_of(me * rows, 128), rows)
        own_text = text_all[pl.ds(pl.multiple_of(me * rows, 16), rows), :]
        exp_texts = jnp.exp(tile_logits(scale, own_text, image_all[...]))
        inv_row = 1.0 / jnp.concatenate(
            [stats[b, :, pairs : pairs + rows] for b in range(n)], axis=1
        )
        inv_own = jnp.broadcast_to(inv_cols[:, own], (rows, rows)).T[:, 0:1]
        coef = exp_texts * (inv_own + inv_row) - 2.0 * label
        acc = jnp.dot(
            coef.astype(jnp.bfloat16), image_all[...], preferred_element_type=jnp.float32
        )
        text_grad_ref[...] = norm_backward(txt_emb, txt_inv, scale * acc)
        stores[1].start()

    def feat_side():
        feat_grad_ref[...] = lax.dot_general(
            img_emb_grad, head_all[...], ROWS_ROWS, preferred_element_type=jnp.float32
        ).astype(jnp.bfloat16)
        stores[0].start()

    for m in range(messages):
        grad_send(m)
        if m >= 1 and image_sent < messages:
            gather_send(IMAGE, image_sent)
            image_sent += 1

    feat_side()
    gather_last(IMAGE)
    text_side()
    total = [head_part(me, pl.ds(0, half)), head_part(me, pl.ds(half, half))]
    for m in range(messages - 2, messages):
        for way in (1, -1):
            grad_copy(way, m).wait_recv()
            which = columns(way, m).start // half
            total[which] += incoming[0 if way == 1 else 1, m].astype(jnp.float32)
    head_grad_ref[:, 0:half] = total[0]
    head_grad_ref[:, half:width] = total[1]
    stores[2].start()

    for m in range(messages):
        for way in (1, -1):
            for kind in gathered:
                gather_copy(kind, way, m, m // 2).wait_send()
            grad_copy(way, m).wait_send()
    for k in range(1, n):
        stats_copy(k, me).wait_send()
    for store in stores:
        store.wait()


def hand_on_kernel(*refs):
    sources, results, held, sem = refs[:3], refs[3:6], refs[6:9], refs[9]
    loads, stores = [], []
    for part in range(2):
        for i in range(3):
            size = held[i].shape[0] // 2
            at = pl.ds(part * size, size)
            k = 3 * part + i
            loads.append(
                pltpu.make_async_copy(sources[i].at[at, :], held[i].at[at, :], sem.at[0, k])
            )
            stores.append(
                pltpu.make_async_copy(held[i].at[at, :], results[i].at[at, :], sem.at[1, k])
            )
    for load in loads:
        load.start()
    for load, store in zip(loads, stores):
        load.wait()
        store.start()
    for store in stores:
        store.wait()


def local_kernel(n, image_features, text_embed, image_head, logit_scale):
    rows, width = text_embed.shape
    depth, feat = image_head.shape[0], image_features.shape[1]
    pairs = n * rows
    half = width // 2
    bf16, f32 = jnp.bfloat16, jnp.float32
    hbm = pl.BlockSpec(memory_space=pltpu.HBM)
    out_shape = (
        jax.ShapeDtypeStruct((rows, feat), bf16),
        jax.ShapeDtypeStruct((rows, width), bf16),
        jax.ShapeDtypeStruct((depth, width), f32),
    )
    results = pl.pallas_call(
        functools.partial(step_kernel, n),
        out_shape=out_shape,
        in_specs=[hbm, hbm, hbm, pl.BlockSpec(memory_space=pltpu.SMEM)],
        out_specs=(hbm, hbm, hbm),
        scratch_shapes=[
            pltpu.VMEM((rows, feat), bf16),
            pltpu.VMEM((rows, width), bf16),
            pltpu.VMEM((depth, width), f32),
            pltpu.VMEM((n * depth, width), bf16),
            pltpu.VMEM((pairs, width), bf16),
            pltpu.VMEM((pairs, width), bf16),
            pltpu.VMEM((n, rows, depth), bf16),
            pltpu.VMEM((n, depth, rows), bf16),
            pltpu.VMEM((rows, feat), bf16),
            pltpu.VMEM((rows, width), bf16),
            pltpu.VMEM((n, rows, rows), f32),
            pltpu.VMEM((n, 1, pairs + rows), f32),
            pltpu.VMEM((1, pairs), f32),
            pltpu.VMEM((2, n - 1, depth, half), bf16),
            pltpu.VMEM((2, n - 1, depth, half), bf16),
            pltpu.SemaphoreType.DMA((3,)),
            pltpu.SemaphoreType.DMA((3,)),
            pltpu.SemaphoreType.DMA((4, 2, n - 1)),
            pltpu.SemaphoreType.DMA((4, 2, n - 1)),
            pltpu.SemaphoreType.DMA((n - 1,)),
            pltpu.SemaphoreType.DMA((n - 1,)),
        ],
        compiler_params=pltpu.CompilerParams(
            collective_id=0, has_side_effects=True, vmem_limit_bytes=62 * 2**20
        ),
    )(image_features, text_embed, image_head, logit_scale)
    return pl.pallas_call(
        hand_on_kernel,
        out_shape=out_shape,
        in_specs=[hbm, hbm, hbm],
        out_specs=(hbm, hbm, hbm),
        scratch_shapes=[
            pltpu.VMEM((rows, feat), bf16),
            pltpu.VMEM((rows, width), bf16),
            pltpu.VMEM((depth, width), f32),
            pltpu.SemaphoreType.DMA((2, 6)),
        ],
        compiler_params=pltpu.CompilerParams(vmem_limit_bytes=62 * 2**20),
    )(*results)


def fits_kernel(n, rows, width, depth, feat):
    pairs = n * rows
    size = 24 * pairs * rows + 4 * pairs * width + 8 * n * depth * width + 12 * rows * feat
    return (
        n % 2 == 0
        and n >= 8
        and rows % 128 == 0
        and width % 256 == 0
        and depth % 16 == 0
        and feat == n * depth
        and size <= 24 * 2**20
    )


def solution(mesh):
    n = mesh.shape["dp"]
    groups = mesh.shape["rep"] * n

    def step(image_features, text_embed, image_head, logit_scale):
        rows, width = text_embed.shape[0] // groups, text_embed.shape[1]
        depth, feat = image_head.shape[0] // groups, image_features.shape[1]
        if fits_kernel(n, rows, width, depth, feat):
            body = functools.partial(local_kernel, n)
        else:
            body = local
        split = P(("rep", "dp"), None)
        return jax.shard_map(
            body,
            mesh=mesh,
            in_specs=(split, split, split, P()),
            out_specs=(split, split, split),
            check_vma=False,
        )(image_features, text_embed, image_head, logit_scale)

    return step
```
